256 devices in a mesh: pool: 4 (over z_lo), row: 16 (over y, x), col: 4 (over z_hi, core).
Axes of the slice: x: 4, y: 4, z: 8 (z_hi: 2, z_lo: 4; z = z_hi * 4 + z_lo), core: 2. Of those that a mesh axis runs over, the one named last changes fastest.
Arguments:
- valence_bands: bfloat16 [4, 2, 48, 2304], P('pool'), may hold values from -6 to 6
- conduction_bands: bfloat16 [512, 2, 48, 2304], P(('pool', 'row', 'col')), may hold values from -6 to 6
- valence_level_energy: float32 [4], replicated, may hold values from -12 to -2
- conduction_energy: float32 [512], P(('pool', 'row', 'col')), may hold values from 2 to 20
- g_index: int32 [5120], replicated, may hold values from 0 to 110591, as said below
Outputs:
- chi_real: float32 [5120, 5120], P(('pool', 'row'), 'col')
- chi_imag: float32 [5120, 5120], P(('pool', 'row'), 'col')
The draws below stay inside these ranges and needn't reach their ends.
Inputs may be any that keep to these rules, and one draw needn't show every extreme that they name: `g_index`: the 5120 entries are distinct, and the indices 0 and 48**3 - 1 always occur.
All inputs are finite; a program needn't handle non-finite values.
Results may differ from the reference program's by a relative error of at most 0.012.
The reference program's roundings to bfloat16 on the way count: a program that leaves them out, or rounds other values in their place, can miss the bound.
Values may be sent and summed in bfloat16 or wider, within the bound.
No kernel may reach another device: no remote copies, remote signals or barrier semaphores. Data moves between devices by JAX's collectives and lax.ppermute only.
A program may use at most 256 MiB of HBM per device.

```python
import math
import jax
import jax.numpy as jnp
from jax import lax

NGRID = 48
NPW = 5120
NV = 4
NCOND = 512


def draw_g_index(key, part):
    key = jax.random.fold_in(key, 7)
    first_key, second_key = jax.random.split(key)
    interior = jax.random.permutation(first_key, NGRID ** 3 - 2)[:NPW - 2] + 1
    chosen = jnp.concatenate([jnp.array([0, NGRID ** 3 - 1], jnp.int32), interior.astype(jnp.int32)])
    return jax.random.permutation(second_key, chosen).astype(jnp.int32)


def levels(rng, dims, cuts, least, top_value):
    gain, own = 1.0, jax.random.fold_in(rng, 6)
    for dim, parts in cuts:
        draws = jnp.exp(jax.random.uniform(jax.random.fold_in(own, dim), (parts,), jnp.float32, least / len(cuts), top_value / len(cuts)))
        gain = gain * jnp.repeat(draws, dims[dim] // parts).reshape([-1 if axis == dim else 1 for axis in range(len(dims))])
    return gain


def normal_values(key, dims, spread, reach, cuts=(), held_as=jnp.bfloat16):
    loudness = levels(key, dims, cuts, -0.22, 0.18) if cuts else 1.0
    result = jax.random.normal(key, dims, jnp.float32) * spread * loudness
    return jnp.minimum(jnp.maximum(result, -reach), reach).astype(held_as)


def setup_inputs(seed: int = 0) -> dict:
    keys = jax.random.split(jax.random.key(seed), 6)
    valence_bands = normal_values(keys[0], (NV, 2, NGRID, NGRID * NGRID), 1.0, 6.0, ((0, 4),))
    conduction_bands = normal_values(keys[1], (NCOND, 2, NGRID, NGRID * NGRID), 1.0, 6.0, ((0, 256),))
    valence_level_energy = jnp.clip(jax.random.uniform(keys[2], (NV,), jnp.float32, -12.0, -2.0), -12.0, -2.0)
    conduction_energy = jnp.clip(2.0 + 18.0 * jax.random.uniform(keys[3], (NCOND,), jnp.float32) ** levels(keys[3], (NCOND,), ((0, 256),), -0.2, 0.2), 2.0, 20.0)
    g_index = draw_g_index(jax.random.fold_in(keys[5], 71), 0)
    return dict(valence_bands=valence_bands, conduction_bands=conduction_bands, valence_level_energy=valence_level_energy, conduction_energy=conduction_energy, g_index=g_index)


def dft_tables(length):
    indices = jnp.arange(length, dtype=jnp.int32)
    product = indices[:, None] * indices[None, :] % length
    angles = product.astype(jnp.float32) * (2.0 * math.pi / length)
    factor = 1.0 / math.sqrt(length)
    return ((jnp.cos(angles) * factor).astype(jnp.bfloat16), (jnp.sin(angles) * factor).astype(jnp.bfloat16))

def axis_step(fields, cos_tab, sin_tab, form):
    real_part = fields[:, 0].astype(jnp.float32)
    imag_part = fields[:, 1].astype(jnp.float32)
    cosine_complete = cos_tab.astype(jnp.float32)
    sin_full = sin_tab.astype(jnp.float32)

    def contract(values, table):
        return jnp.einsum(form, values, table, precision=lax.Precision.HIGHEST)
    new_real = contract(real_part, cosine_complete) + contract(imag_part, sin_full)
    new_imag = contract(imag_part, cosine_complete) - contract(real_part, sin_full)
    return jnp.stack([new_real, new_imag], 1)

def pair_coefficients(valence_bands, val_energy, cond_bands, cond_energy, g_index, scale):
    count_v = valence_bands.shape[0]
    count_c = cond_bands.shape[0]
    grid = valence_bands.shape[2]
    cos_tab, sin_tab = dft_tables(grid)
    val_re = valence_bands[:, 0].astype(jnp.float32)[:, None]
    val_im = valence_bands[:, 1].astype(jnp.float32)[:, None]
    cond_re = cond_bands[:, 0].astype(jnp.float32)[None]
    cond_im = cond_bands[:, 1].astype(jnp.float32)[None]
    rho_re = val_re * cond_re + val_im * cond_im
    pair_density_imaginary = val_re * cond_im - val_im * cond_re
    density = jnp.stack([rho_re, pair_density_imaginary], 2).astype(jnp.bfloat16)
    density = density.reshape(count_v * count_c, 2, grid, grid, grid)
    section = axis_step(density, cos_tab, sin_tab, 'bxyn,kn->bxyk').astype(jnp.bfloat16)
    section = axis_step(section, cos_tab, sin_tab, 'bxnz,kn->bxkz').astype(jnp.bfloat16)
    final = axis_step(section, cos_tab, sin_tab, 'bnyz,kn->bkyz')
    flat = final.reshape(count_v * count_c, 2, grid * grid * grid)
    coeffs = jnp.take(flat, g_index, axis=2)
    pair_weight_factors = 2.0 / ((val_energy[:, None] - cond_energy[None, :]) * scale)
    pair_weight_factors = pair_weight_factors.reshape(count_v * count_c, 1, 1)
    weighted = (pair_weight_factors * coeffs).astype(jnp.bfloat16)
    plain = coeffs.astype(jnp.bfloat16)
    return jnp.stack([weighted, plain], 1)

def reference(valence_bands, conduction_bands, valence_level_energy, conduction_energy, g_index):
    scale = math.sqrt(NV * NCOND)

    def one_band(inputs):
        band, energy = inputs
        return pair_coefficients(valence_bands, valence_level_energy, band[None], energy[None], g_index, scale)
    stacked = lax.map(one_band, (conduction_bands, conduction_energy))
    stacked = stacked.reshape(NCOND * NV, 2, 2, NPW)
    weighted = stacked[:, 0].astype(jnp.float32)
    plain = stacked[:, 1].astype(jnp.float32)
    right_im = jnp.stack([-plain[:, 1], plain[:, 0]], 1)
    right = jnp.concatenate([plain, right_im], 2)
    left = weighted.reshape(NCOND * NV * 2, NPW)
    right = right.reshape(NCOND * NV * 2, 2 * NPW)
    chi = jnp.dot(left.T, right, precision=lax.Precision.HIGHEST, preferred_element_type=jnp.float32)
    return (chi[:, :NPW], chi[:, NPW:])
```

```python
import functools
import math

import jax
import jax.numpy as jnp
import ml_dtypes
import numpy as np
from jax import lax
from jax.experimental import pallas as pl
from jax.experimental.pallas import tpu as pltpu
from jax.sharding import Mesh, PartitionSpec as P

NV = 4
N = 48
NG = 5120
F32 = jnp.float32
BF16 = jnp.bfloat16
AXES = ("p", "y", "x", "h", "c")


def tables():
    k = np.arange(N)
    ang = (k[:, None] * k[None, :] % N).astype(np.float32) * np.float32(2.0 * math.pi / N)
    fac = np.float32(1.0 / math.sqrt(N))
    cos = (np.cos(ang) * fac).astype(ml_dtypes.bfloat16)
    sin = (np.sin(ang) * fac).astype(ml_dtypes.bfloat16)
    return cos, sin


def wide_tables():
    cos, sin = tables()
    cs = cos.astype(np.float32)
    sn = sin.astype(np.float32)
    eye8 = np.eye(8, dtype=np.float32)
    wz = np.zeros((2, 8, 48, 2, 48, 8), np.float32)
    for (f, g, tab) in ((0, 0, cs), (1, 0, sn), (0, 1, -sn), (1, 1, cs)):
        wz[f, :, :, g] = np.einsum("ab,kz->azkb", eye8, tab)
    wz = wz.reshape(768, 768)
    eye16 = np.eye(16, dtype=np.float32)
    wy = np.zeros((6, 2, 16, 8, 2, 16, 48), np.float32)
    for (f, g, tab) in ((0, 0, cs), (1, 0, sn), (0, 1, -sn), (1, 1, cs)):
        t = tab.reshape(48, 6, 8)
        wy[:, f, :, :, g] = np.einsum("ab,kmi->maibk", eye16, t)
    wy = wy.reshape(1536, 1536)
    return wz.astype(ml_dtypes.bfloat16), wy.astype(ml_dtypes.bfloat16), cos, sin


def coeff_kernel(core, own, part, other, cond, wz, wy, tc, ts, q, kx, w, left, right, xs, zs, s, oh, m):
    first = core[0] == 0

    def zstep(i, _):
        cols = pl.ds(pl.multiple_of(i * 384, 128), 384)
        for v in range(NV):
            if v == 0:
                vr = own[0, 0, :, cols].astype(F32)
                vi = own[0, 1, :, cols].astype(F32)
            else:
                a = part[v - 1, :, cols].astype(F32)
                b = other[v - 1, :, cols].astype(F32)
                vr = jnp.where(first, a, b)
                vi = jnp.where(first, b, a)
            for c in range(2):
                cr = cond[c, 0, :, cols].astype(F32)
                ci = cond[c, 1, :, cols].astype(F32)
                rows = slice((v * 2 + c) * N, (v * 2 + c + 1) * N)
                xs[rows, 0:384] = (vr * cr + vi * ci).astype(BF16)
                xs[rows, 384:768] = (vr * ci - vi * cr).astype(BF16)
        z = jnp.dot(xs[...], wz[...], preferred_element_type=F32).astype(BF16)
        for t in range(3):
            for f in range(2):
                zs[t, :, pl.ds(pl.multiple_of((i * 2 + f) * 128, 128), 128)] = z[
                    :, f * 384 + t * 128 : f * 384 + (t + 1) * 128
                ]
        return 0

    lax.fori_loop(0, 6, zstep, 0)

    def ystep(t, _):
        for f in range(2):
            out = jnp.dot(zs[t], wy[:, f * 768 : (f + 1) * 768], preferred_element_type=F32)
            s[f * 384 : (f + 1) * 384, pl.ds(pl.multiple_of(t * 768, 128), 768)] = out.astype(BF16)
        return 0

    lax.fori_loop(0, 3, ystep, 0)

    def gstep(n, _):
        cols = pl.ds(pl.multiple_of(n * 256, 128), 256)
        qq = q[:, cols]
        rows = lax.broadcasted_iota(jnp.int32, (128, 256), 0)
        for k in range(18):
            oh[k * 128 : (k + 1) * 128] = jnp.where(rows == qq - 128 * k, 1.0, 0.0).astype(BF16)
        full = jnp.dot(s[...], oh[...], preferred_element_type=F32).reshape(2, 8, N, 256)
        kk = kx[:, cols]
        ohk = jnp.where(lax.broadcasted_iota(jnp.int32, (N, 256), 0) == kk, 1.0, 0.0).astype(BF16)
        co = jnp.dot(tc[...], ohk, preferred_element_type=F32)
        si = jnp.dot(ts[...], ohk, preferred_element_type=F32)
        m[0, :, cols] = jnp.sum(full[0] * co + full[1] * si, axis=1)
        m[1, :, cols] = jnp.sum(full[1] * co - full[0] * si, axis=1)
        return 0

    lax.fori_loop(0, 20, gstep, 0)

    for z in range(8):
        for f in range(2):
            right[z, :, f * 640 : (f + 1) * 640] = m[f, :, z * 640 : (z + 1) * 640].astype(BF16)
    weight = w[...]
    for r in range(16):
        parts = []
        for f in range(2):
            for b in range(4):
                lane = ((b // 2 * 4 + r // 4) * 2 + b % 2) * 320 + 80 * (r % 4)
                parts.append(m[f, :, lane : lane + 80])
        left[r] = (weight * jnp.concatenate(parts, axis=1)).astype(BF16)


def coefficients(core, own, part, other, cond, q, kx, w):
    wz, wy, cos, sin = wide_tables()
    vm = pl.BlockSpec(memory_space=pltpu.VMEM)
    sm = pl.BlockSpec(memory_space=pltpu.SMEM)
    return pl.pallas_call(
        coeff_kernel,
        out_shape=(
            jax.ShapeDtypeStruct((16, 8, 640), BF16),
            jax.ShapeDtypeStruct((8, 8, 1280), BF16),
        ),
        in_specs=[sm] + [vm] * 11,
        out_specs=(vm, vm),
        scratch_shapes=[
            pltpu.VMEM((384, 768), BF16),
            pltpu.VMEM((3, 384, 1536), BF16),
            pltpu.VMEM((768, 2304), BF16),
            pltpu.VMEM((2304, 256), BF16),
            pltpu.VMEM((2, 8, NG), F32),
        ],
        compiler_params=pltpu.CompilerParams(vmem_limit_bytes=48 * 2**20),
    )(core, own, part, other, cond, jnp.asarray(wz), jnp.asarray(wy), jnp.asarray(cos), jnp.asarray(sin), q, kx, w)


def chi_kernel(core, place, rows, l0, l1, l2, l3, r0, r1, r2, r3, r4, mine, theirs, lall, lk, rk):
    for i, piece in enumerate((l0, l1, l2, l3)):
        lall[2 * i : 2 * i + 2] = piece[...]
    base = 0
    for piece in (r0, r1, r2, r3, r4):
        size = piece.shape[0]
        rk[base : base + size] = piece[...]
        base += size

    def fill(k, _):
        r = rows[k]
        for u in range(4):
            pair = [lall[place[2 * u + e], r].astype(F32) for e in range(2)]
            lk[pl.ds(pl.multiple_of(k * 64 + u * 16, 16), 16), :] = jnp.concatenate(pair, axis=0).astype(BF16)
        return 0

    lax.fori_loop(0, 16, fill, 0)
    first = core[0] == 0
    half = 320

    def product(f):
        return lax.dot_general(
            lk[:, f * half : (f + 1) * half], rk[...], (((0,), (0,)), ((), ())), preferred_element_type=F32
        )

    re = product(0)
    im = product(1)
    chi_re = re[:, :640] + im[:, 640:]
    chi_im = im[:, :640] - re[:, 640:]
    for k, chi in enumerate((chi_re, chi_im)):
        a, b = chi[:, :half], chi[:, half:]
        cols = slice(k * half, (k + 1) * half)
        mine[:, cols] = jnp.where(first, a, b)
        theirs[:, cols] = jnp.where(first, b, a)


def chi_tiles(core, place, rows, lefts, rights):
    vm = pl.BlockSpec(memory_space=pltpu.VMEM)
    sm = pl.BlockSpec(memory_space=pltpu.SMEM)
    return pl.pallas_call(
        chi_kernel,
        out_shape=(jax.ShapeDtypeStruct((320, 640), F32),) * 2,
        in_specs=[sm] * 3 + [vm] * 9,
        out_specs=(vm, vm),
        scratch_shapes=[
            pltpu.VMEM((8, 16, 8, 640), BF16),
            pltpu.VMEM((1024, 640), BF16),
            pltpu.VMEM((1024, 1280), BF16),
        ],
        compiler_params=pltpu.CompilerParams(vmem_limit_bytes=48 * 2**20),
    )(core, place, rows, *lefts, *rights)


def send(values, target):
    def index(z, y, x, c):
        return ((((z % 4) * 4 + y % 4) * 4 + x % 4) * 2 + (z % 8) // 4) * 2 + c

    pairs = [
        (index(z, y, x, c), index(*target(z, y, x, c)))
        for z in range(8)
        for y in range(4)
        for x in range(4)
        for c in range(2)
    ]
    return lax.ppermute(values, AXES, pairs)


def send_z(values, step):
    return send(values, lambda z, y, x, c: (z + step, y, x, c))


def send_core(values):
    return send(values, lambda z, y, x, c: (z, y, x, 1 - c))


def plane(axis, move):
    def target(z, y, x, c):
        if axis == c:
            return z, y, move(x), c
        return z, move(y), x, c

    return target


def outward(a):
    return a + 1 if a % 2 else a - 1


def inward(a):
    return a ^ 1


def ring(move):
    def target(z, y, x, c):
        return (move((z - c) % 8) + c) % 8, y, x, c

    return target


def ordered(flag, one, two):
    return jnp.where(flag, jnp.concatenate([one, two]), jnp.concatenate([two, one]))


def local(valence, conduction, valence_energy, conduction_energy, g_index):
    p, y, x, h, c = (lax.axis_index(a) for a in AXES)
    z = h * 4 + p
    core = jnp.reshape(c, (1,)).astype(jnp.int32)

    piece = lax.dynamic_index_in_dim(valence[0], c, 0, keepdims=False)
    part = jnp.concatenate(
        [
            send_z(piece, -1)[None],
            send_z(piece, 1)[None],
            jnp.concatenate([send_z(piece[:32], 2), send_z(piece[32:], -2)])[None],
        ]
    )
    other = send_core(part)
    bands = (p + jnp.array([0, 1, 3, 2])) % NV

    scale = math.sqrt(NV * 512)
    weight = 2.0 / ((valence_energy[bands][:, None] - conduction_energy[None, :]) * scale)
    order = g_index.reshape(2, 2, 4, 320).transpose(0, 2, 1, 3).reshape(1, NG)
    column = order % (N * N)
    left, right = coefficients(
        core,
        valence,
        part,
        other,
        conduction,
        (column % N) * N + column // N,
        order // (N * N),
        weight.reshape(8, 1),
    )

    right = lax.all_to_all(right, ("h", "p"), 0, 0, tiled=True).reshape(64, 1280)
    left = lax.all_to_all(left, ("y", "x"), 0, 0, tiled=True)[None]

    a = jnp.where(c == 0, x, y)
    b = jnp.where(c == 0, y, x)
    two = ordered(a % 2 == 0, right, send(right, plane(0, inward)))
    four = ordered(a < 2, two, send(two, plane(0, outward)))
    up = send(four, plane(1, lambda i: i + 1))
    down = send(four, plane(1, lambda i: i - 1))
    far_low = send(up[:128], plane(1, lambda i: i + 1))
    far_high = send(down[128:], plane(1, lambda i: i - 1))
    rights = (four, up, down, far_low, far_high)
    step = jnp.array([0, 3, 1, 2])
    bb = jnp.repeat((b + step) % 4, 4)
    aa = jnp.tile(jnp.arange(4), 4)
    rows = jnp.where(c == 0, bb * 4 + aa, aa * 4 + bb).astype(jnp.int32)

    zz = (z - c) % 8
    odd = zz % 2
    left0 = ordered(odd == 0, left, send(left, ring(inward)))
    left1 = send(left0, ring(outward))
    left2 = send(left1, ring(inward))
    left3 = send(left2, ring(outward))
    sign = 2 * odd - 1
    blocks = (zz // 2 + jnp.stack([0 * odd, sign, -sign, 0 * odd + 2])) % 4
    held = (jnp.stack([2 * blocks, 2 * blocks + 1], 1).reshape(8) + c) % 8
    place = jnp.argmax(held[None, :] == jnp.arange(8)[:, None], axis=1).astype(jnp.int32)

    mine, theirs = chi_tiles(core, place, rows, (left0, left1, left2, left3), rights)
    tile = (mine + send_core(theirs)).astype(BF16).reshape(4, 80, 640)
    tile = lax.all_to_all(tile, "p", 0, 0, tiled=True)
    full = jnp.transpose(tile.reshape(4, 80, 2, 320), (2, 1, 0, 3)).reshape(2, 80, 1280).astype(F32)
    return full[0], full[1]


def solution(mesh):
    fine = Mesh(mesh.devices.reshape(4, 4, 4, 2, 2), AXES)
    bands = P(AXES)
    return jax.shard_map(
        local,
        mesh=fine,
        in_specs=(P("p"), bands, P(), bands, P()),
        out_specs=(P(("p", "y", "x"), ("h", "c")),) * 2,
        check_vma=False,
    )
```

```python
import functools
import math

import jax
import jax.numpy as jnp
import ml_dtypes
import numpy as np
from jax import lax
from jax.experimental import pallas as pl
from jax.experimental.pallas import tpu as pltpu
from jax.sharding import Mesh, PartitionSpec as P

NV = 4
N = 48
NG = 5120
F32 = jnp.float32
BF16 = jnp.bfloat16
WINDOW = 256
GROUP = 4
AXES = ("p", "y", "x", "h", "c")


def tables():
    k = np.arange(N)
    ang = (k[:, None] * k[None, :] % N).astype(np.float32) * np.float32(2.0 * math.pi / N)
    fac = np.float32(1.0 / math.sqrt(N))
    cos = (np.cos(ang) * fac).astype(ml_dtypes.bfloat16)
    sin = (np.sin(ang) * fac).astype(ml_dtypes.bfloat16)
    return cos, sin


def wide_tables():
    cos, sin = tables()
    cs = cos.astype(np.float32)
    sn = sin.astype(np.float32)
    eye8 = np.eye(8, dtype=np.float32)
    wz = np.zeros((2, 8, 48, 2, 48, 8), np.float32)
    for (f, g, tab) in ((0, 0, cs), (1, 0, sn), (0, 1, -sn), (1, 1, cs)):
        wz[f, :, :, g] = np.einsum("ab,kz->azkb", eye8, tab)
    wz = wz.reshape(768, 768)
    eye16 = np.eye(16, dtype=np.float32)
    wy = np.zeros((6, 16, 8, 2, 16, 24), np.float32)
    half = sn[:24].copy()
    half[0] = cs[24]
    for j, tab in enumerate((cs[:24], half)):
        wy[:, :, :, j] = np.einsum("ab,kmi->maibk", eye16, tab.reshape(24, 6, 8))
    wy = wy.reshape(768, 768)
    return wz.astype(ml_dtypes.bfloat16), wy.astype(ml_dtypes.bfloat16), cos, sin


def column_of(y, z):
    slot = jnp.where(y < 24, y, 24 + (N - y) % 24)
    return (z // 16) * 768 + (slot // 24) * 384 + (z % 16) * 24 + slot % 24


def densities(val, cond, cols, xs, k):
    for v in range(len(val)):
        vr, vi = val[v](cols)
        for c in range(2):
            cr = cond[c, 0, :, cols].astype(F32)
            ci = cond[c, 1, :, cols].astype(F32)
            rows = slice((v * 2 + c) * N, (v * 2 + c + 1) * N)
            xs[k, rows, 0:384] = (vr * cr + vi * ci).astype(BF16)
            xs[k, rows, 384:768] = (vr * ci - vi * cr).astype(BF16)


def sections(val, cond, wz, wy, xs, zs, s):
    count = zs.shape[1] // 2
    for i in range(6):
        densities(val, cond, slice(i * 384, (i + 1) * 384), xs, i % 2)
        out = jnp.dot(xs[i % 2], wz[...], preferred_element_type=F32).astype(BF16)
        for t in range(3):
            for f in range(2):
                zs[t, f * count : (f + 1) * count, i * 128 : (i + 1) * 128] = out[
                    :, f * 384 + t * 128 : f * 384 + (t + 1) * 128
                ]
    edge = lax.broadcasted_iota(jnp.int32, (1, 384), 1) % 24 == 0
    for t in range(3):
        cp = jnp.dot(zs[t], wy[:, :384], preferred_element_type=F32)
        sp = jnp.dot(zs[t], wy[:, 384:], preferred_element_type=F32)
        cre, cim, sre, sim = cp[:count], cp[count:], sp[:count], sp[count:]
        outs = (
            (jnp.where(edge, cre, cre + sim), jnp.where(edge, sre, cre - sim)),
            (jnp.where(edge, cim, cim - sre), jnp.where(edge, sim, cim + sre)),
        )
        for f in range(2):
            for e in range(2):
                cols = slice((t * 2 + e) * 384, (t * 2 + e + 1) * 384)
                s[f * count : (f + 1) * count, cols] = outs[f][e].astype(BF16)
    s[:, N * N :] = jnp.zeros((2 * count, WINDOW), BF16)


def select(s, tc, ts, starts, key, m, row):
    pairs = s.shape[0] // (2 * N)

    def step(group, _):
        todo = []
        for u in range(GROUP):
            n = group * GROUP + u
            cols = pl.ds(pl.multiple_of(n * 256, 128), 256)
            column = key[:, cols] >> 6
            kx = key[:, cols] & 63
            hot = jnp.where(lax.broadcasted_iota(jnp.int32, (N, 256), 0) == kx, 1.0, 0.0).astype(BF16)
            co = jnp.dot(tc[...], hot, preferred_element_type=F32)
            si = jnp.dot(ts[...], hot, preferred_element_type=F32)
            low = (starts[0, n * 256] >> 6) // 128 * 128
            high = starts[0, n * 256 + 255] >> 6

            def window(base, column=column, co=co, si=si):
                rows = lax.broadcasted_iota(jnp.int32, (WINDOW, 256), 0)
                pick = jnp.where(rows == column - base, 1.0, 0.0).astype(BF16)
                part = s[:, pl.ds(pl.multiple_of(base, 128), WINDOW)]
                full = jnp.dot(part, pick, preferred_element_type=F32).reshape(2, pairs, N, 256)
                re = jnp.sum(full[0] * co + full[1] * si, axis=1)
                im = jnp.sum(full[1] * co - full[0] * si, axis=1)
                return re, im

            re, im = window(low)
            m[0, row : row + pairs, cols] = re
            m[1, row : row + pairs, cols] = im
            todo.append((window, low, high, cols))
        for window, low, high, cols in todo:

            def more(k, _, window=window, low=low, cols=cols):
                re, im = window(low + k * WINDOW)
                m[0, row : row + pairs, cols] += re
                m[1, row : row + pairs, cols] += im
                return 0

            lax.fori_loop(1, (high - low) // WINDOW + 1, more, 0)
        return 0

    lax.fori_loop(0, 20 // GROUP, step, 0)


def own_kernel(val, cond, wz, wy, tc, ts, starts, key, m, xs, zs, s):
    def band(cols):
        return val[0, 0, :, cols].astype(F32), val[0, 1, :, cols].astype(F32)

    sections([band], cond, wz, wy, xs, zs, s)
    select(s, tc, ts, starts, key, m, 0)


def rest_kernel(core, part, other, cond, wz, wy, tc, ts, starts, key, back, w, owned, left, right, xs, zs, s, m, mo):
    first = core[0] == 0

    def band(v):
        def read(cols):
            a = part[v, :, cols].astype(F32)
            b = other[v, :, cols].astype(F32)
            return jnp.where(first, a, b), jnp.where(first, b, a)

        return read

    sections([band(v) for v in range(3)], cond, wz, wy, xs, zs, s)
    select(s, tc, ts, starts, key, m, 2)
    m[:, 0:2, :] = owned[...]

    def unsort(group, _):
        for u in range(4):
            cols = pl.ds(pl.multiple_of((group * 4 + u) * 128, 128), 128)
            place = jnp.broadcast_to(back[:, cols], (8, 128))
            source = place >> 7
            lane = place & 127
            outs = [jnp.zeros((8, 128), F32)] * 2
            for k in range(40):
                hit = source == k
                for f in range(2):
                    got = jnp.take_along_axis(m[f, :, k * 128 : (k + 1) * 128], lane, axis=1)
                    outs[f] = jnp.where(hit, got, outs[f])
            for f in range(2):
                mo[f, :, cols] = outs[f]
        return 0

    lax.fori_loop(0, 10, unsort, 0)
    for z in range(8):
        for f in range(2):
            right[z, :, f * 640 : (f + 1) * 640] = mo[f, :, z * 640 : (z + 1) * 640].astype(BF16)
    weight = w[...]
    for r in range(16):
        parts = []
        for f in range(2):
            for b in range(4):
                lane = ((b // 2 * 4 + r // 4) * 2 + b % 2) * 320 + 80 * (r % 4)
                parts.append(mo[f, :, lane : lane + 80])
        left[r] = (weight * jnp.concatenate(parts, axis=1)).astype(BF16)


VM = pl.BlockSpec(memory_space=pltpu.VMEM)
SM = pl.BlockSpec(memory_space=pltpu.SMEM)


def scratch(pairs):
    rows = pairs * N
    return [
        pltpu.VMEM((2, rows, 768), BF16),
        pltpu.VMEM((3, 2 * rows, 768), BF16),
        pltpu.VMEM((2 * rows, N * N + WINDOW), BF16),
    ]


def own_coefficients(val, cond, wide, key):
    return pl.pallas_call(
        own_kernel,
        out_shape=jax.ShapeDtypeStruct((2, 2, NG), F32),
        in_specs=[VM] * 6 + [SM, VM],
        out_specs=VM,
        scratch_shapes=scratch(2),
        compiler_params=pltpu.CompilerParams(vmem_limit_bytes=40 * 2**20),
        cost_estimate=pl.CostEstimate(flops=5 * 10**9, bytes_accessed=3 * 10**7, transcendentals=0),
    )(val, cond, *wide, key, key)


def coefficients(core, part, other, cond, wide, key, back, w, owned):
    return pl.pallas_call(
        rest_kernel,
        out_shape=(
            jax.ShapeDtypeStruct((16, 8, 640), BF16),
            jax.ShapeDtypeStruct((8, 8, 1280), BF16),
        ),
        in_specs=[SM] + [VM] * 7 + [SM] + [VM] * 4,
        out_specs=(VM, VM),
        scratch_shapes=scratch(6) + [pltpu.VMEM((2, 8, NG), F32)] * 2,
        compiler_params=pltpu.CompilerParams(vmem_limit_bytes=40 * 2**20),
        cost_estimate=pl.CostEstimate(flops=10**10, bytes_accessed=5 * 10**7, transcendentals=0),
    )(core, part, other, cond, *wide, key, key, back, w, owned)


def chi_kernel(core, place, rows, l0, l1, l2, l3, r0, r1, r2, r3, mine, theirs, lall, lk, rk):
    for i, piece in enumerate((l0, l1, l2, l3)):
        lall[2 * i : 2 * i + 2] = piece[...]
    base = 0
    for piece in (r0, r1, r2, r3):
        size = piece.shape[0]
        rk[base : base + size] = piece[...]
        base += size

    def fill(k, _):
        r = rows[k]
        for u in range(4):
            pair = [lall[place[2 * u + e], r].astype(F32) for e in range(2)]
            lk[pl.ds(pl.multiple_of(k * 64 + u * 16, 16), 16), :] = jnp.concatenate(pair, axis=0).astype(BF16)
        return 0

    lax.fori_loop(0, 16, fill, 0)
    first = core[0] == 0
    half = 320

    def product(f):
        return lax.dot_general(
            lk[:, f * half : (f + 1) * half], rk[...], (((0,), (0,)), ((), ())), preferred_element_type=F32
        )

    re = product(0)
    im = product(1)
    chi_re = re[:, :640] + im[:, 640:]
    chi_im = im[:, :640] - re[:, 640:]
    for k, chi in enumerate((chi_re, chi_im)):
        a, b = chi[:, :half], chi[:, half:]
        cols = slice(k * half, (k + 1) * half)
        mine[:, cols] = jnp.where(first, a, b)
        theirs[:, cols] = jnp.where(first, b, a)


def chi_tiles(core, place, rows, lefts, rights):
    vm = pl.BlockSpec(memory_space=pltpu.VMEM)
    sm = pl.BlockSpec(memory_space=pltpu.SMEM)
    return pl.pallas_call(
        chi_kernel,
        out_shape=(jax.ShapeDtypeStruct((320, 640), F32),) * 2,
        in_specs=[sm] * 3 + [vm] * 8,
        out_specs=(vm, vm),
        scratch_shapes=[
            pltpu.VMEM((8, 16, 8, 640), BF16),
            pltpu.VMEM((1024, 640), BF16),
            pltpu.VMEM((1024, 1280), BF16),
        ],
        compiler_params=pltpu.CompilerParams(vmem_limit_bytes=48 * 2**20),
    )(core, place, rows, *lefts, *rights)


def send(values, target):
    def index(z, y, x, c):
        return ((((z % 4) * 4 + y % 4) * 4 + x % 4) * 2 + (z % 8) // 4) * 2 + c

    pairs = [
        (index(z, y, x, c), index(*target(z, y, x, c)))
        for z in range(8)
        for y in range(4)
        for x in range(4)
        for c in range(2)
    ]
    return lax.ppermute(values, AXES, pairs)


def send_z(values, step):
    return send(values, lambda z, y, x, c: (z + step, y, x, c))


def send_core(values):
    return send(values, lambda z, y, x, c: (z, y, x, 1 - c))


def plane(axis, move):
    def target(z, y, x, c):
        if axis == c:
            return z, y, move(x), c
        return z, move(y), x, c

    return target


def outward(a):
    return a + 1 if a % 2 else a - 1


def inward(a):
    return a ^ 1


def ring(move):
    def target(z, y, x, c):
        return (move((z - c) % 8) + c) % 8, y, x, c

    return target


def assemble_kernel(tile, re, im):
    for f, out in enumerate((re, im)):
        parts = [tile[k, :, f * 320 : (f + 1) * 320].astype(F32) for k in range(4)]
        out[...] = jnp.concatenate(parts, axis=1)


def assemble(tile):
    return pl.pallas_call(
        assemble_kernel,
        out_shape=(jax.ShapeDtypeStruct((80, 1280), F32),) * 2,
        in_specs=[VM],
        out_specs=(VM, VM),
    )(tile)


def local(valence, conduction, valence_energy, conduction_energy, g_index):
    p, y, x, h, c = (lax.axis_index(a) for a in AXES)
    z = h * 4 + p
    core = jnp.reshape(c, (1,)).astype(jnp.int32)

    piece = lax.dynamic_index_in_dim(valence[0], c, 0, keepdims=False)
    part = jnp.concatenate(
        [
            send_z(piece, -1)[None],
            send_z(piece, 1)[None],
            jnp.concatenate([send_z(piece[:32], 2), send_z(piece[32:], -2)])[None],
        ]
    )
    other = send_core(part)
    bands = (p + jnp.array([0, 1, 3, 2])) % NV
    scale = math.sqrt(NV * 512)
    weight = 2.0 / ((valence_energy[bands][:, None] - conduction_energy[None, :]) * scale)

    order = g_index.reshape(2, 2, 4, 320).transpose(0, 2, 1, 3).reshape(NG)
    plane_part = order % (N * N)
    key = (column_of(plane_part // N, plane_part % N) << 6) | (order // (N * N))
    lanes = lax.iota(jnp.int32, NG)
    key, perm = lax.sort((key, lanes), num_keys=1)
    back = lax.sort((perm << 13) | lanes) & 8191
    key = key.reshape(1, NG)

    wide = [jnp.asarray(t) for t in wide_tables()]
    owned = own_coefficients(valence, conduction, wide, key)
    left, right = coefficients(
        core, part, other, conduction, wide, key, back.reshape(1, NG), weight.reshape(8, 1), owned
    )

    left = lax.all_to_all(left, ("y", "x"), 0, 0, tiled=True)
    left, right = lax.optimization_barrier((left, right))
    right = lax.all_to_all(right, ("h", "p"), 0, 0, tiled=True).reshape(64, 1280)

    zz = (z - c) % 8
    left0 = jnp.stack([left, send(left, ring(inward))])
    left1 = send(left0, ring(outward))
    left2 = send(left1, ring(inward))
    left3 = send(left2, ring(outward))
    near = zz ^ 1
    one = (zz + 2 * (zz % 2) - 1) % 8
    two = (near + 2 * (near % 2) - 1) % 8
    three = ((one ^ 1) + 2 * ((one ^ 1) % 2) - 1) % 8
    held = jnp.stack([zz, near, one, one ^ 1, two, two ^ 1, three, three ^ 1])
    held = (held + c) % 8
    place = jnp.argmax(held[None, :] == jnp.arange(8)[:, None], axis=1).astype(jnp.int32)

    moves = (lambda i: i + 1, lambda i: i - 1, lambda i: i + 2)
    offsets = jnp.array([0, 3, 1, 2])
    four = jnp.concatenate([right] + [send(right, plane(0, move)) for move in moves])
    rights = [four] + [send(four, plane(1, move)) for move in moves]
    aa = jnp.tile((jnp.where(c == 0, x, y) + offsets) % 4, 4)
    bb = jnp.repeat((jnp.where(c == 0, y, x) + offsets) % 4, 4)
    rows = jnp.where(c == 0, bb * 4 + aa, aa * 4 + bb).astype(jnp.int32)

    mine, theirs = chi_tiles(core, place, rows, (left0, left1, left2, left3), rights)
    tile = (mine + send_core(theirs)).astype(BF16).reshape(4, 80, 640)
    return assemble(lax.all_to_all(tile, "p", 0, 0, tiled=True))


def solution(mesh):
    fine = Mesh(mesh.devices.reshape(4, 4, 4, 2, 2), AXES)
    bands = P(AXES)
    return jax.shard_map(
        local,
        mesh=fine,
        in_specs=(P("p"), bands, P(), bands, P()),
        out_specs=(P(("p", "y", "x"), ("h", "c")),) * 2,
        check_vma=False,
    )
```

```python
import functools
import math

import jax
import jax.numpy as jnp
import ml_dtypes
import numpy as np
from jax import lax
from jax.experimental import pallas as pl
from jax.experimental.pallas import tpu as pltpu
from jax.sharding import Mesh, PartitionSpec as P

NV = 4
N = 48
NG = 5120
F32 = jnp.float32
BF16 = jnp.bfloat16
WINDOW = 256
GROUP = 4
BUCKETS = 24
VM = pl.BlockSpec(memory_space=pltpu.VMEM)
SM = pl.BlockSpec(memory_space=pltpu.SMEM)
AXES = ("p", "y", "x", "h", "c")


def tables():
    k = np.arange(N)
    ang = (k[:, None] * k[None, :] % N).astype(np.float32) * np.float32(2.0 * math.pi / N)
    fac = np.float32(1.0 / math.sqrt(N))
    cos = (np.cos(ang) * fac).astype(ml_dtypes.bfloat16)
    sin = (np.sin(ang) * fac).astype(ml_dtypes.bfloat16)
    return cos, sin


def wide_tables():
    cos, sin = tables()
    cs = cos.astype(np.float32)
    sn = sin.astype(np.float32)
    eye8 = np.eye(8, dtype=np.float32)
    wz = np.zeros((2, 8, 48, 2, 48, 8), np.float32)
    for (f, g, tab) in ((0, 0, cs), (1, 0, sn), (0, 1, -sn), (1, 1, cs)):
        wz[f, :, :, g] = np.einsum("ab,kz->azkb", eye8, tab)
    wz = wz.reshape(768, 768)
    eye16 = np.eye(16, dtype=np.float32)
    wy = np.zeros((6, 16, 8, 2, 16, 24), np.float32)
    half = sn[:24].copy()
    half[0] = cs[24]
    for j, tab in enumerate((cs[:24], half)):
        wy[:, :, :, j] = np.einsum("ab,kmi->maibk", eye16, tab.reshape(24, 6, 8))
    wy = wy.reshape(768, 768)
    return wz.astype(ml_dtypes.bfloat16), wy.astype(ml_dtypes.bfloat16), cos, sin


def column_of(y, z):
    within = jnp.where(y < 24, y, jnp.where(y == 24, 0, N - y))
    return (z >> 4) * 768 + jnp.where(y < 24, 0, 384) + (z & 15) * 24 + within


def sort_kernel(key, keys, place, held):
    bucket = key[...] >> 13
    slots = lax.broadcasted_iota(jnp.int32, (BUCKETS, 128), 0)
    before = jnp.zeros((BUCKETS, 128), F32)
    for k in range(40):
        mine = bucket[:, k * 128 : (k + 1) * 128]
        held[k] = jnp.where(slots == mine, 1.0, 0.0)
        before += jnp.where(mine < slots, 1.0, 0.0)
    upto = lax.broadcasted_iota(jnp.int32, (128, 128), 0) <= lax.broadcasted_iota(jnp.int32, (128, 128), 1)
    counts = jnp.dot(
        held[...].reshape(40 * BUCKETS, 128).astype(BF16),
        jnp.where(upto, 1.0, 0.0).astype(BF16),
        preferred_element_type=F32,
    ).reshape(40, BUCKETS, 128)
    base = jnp.sum(before, axis=1, keepdims=True) - 1.0
    for k in range(40):
        rank = jnp.sum(held[k] * (base + counts[k]), axis=0, keepdims=True)
        place[:, k * 128 : (k + 1) * 128] = rank.astype(jnp.int32)
        base = base + counts[k, :, 127:128]
    high = place[...] >> 7
    low = place[...] & 127
    at = lax.broadcasted_iota(jnp.int32, (40, NG), 0) == high
    parts = (bucket, (key[...] >> 6) & 127, key[...] & 63)
    rows = jnp.concatenate([jnp.where(at, v.astype(F32), 0.0) for v in parts], axis=0).astype(BF16)
    cols = jnp.where(lax.broadcasted_iota(jnp.int32, (128, NG), 0) == low, 1.0, 0.0).astype(BF16)
    moved = lax.dot_general(rows, cols, (((1,), (1,)), ((), ())), preferred_element_type=F32).astype(jnp.int32)
    keys[...] = (moved[0:40] << 13) | (moved[40:80] << 6) | moved[80:120]


def sort_waves(key):
    return pl.pallas_call(
        sort_kernel,
        out_shape=(jax.ShapeDtypeStruct((40, 128), jnp.int32), jax.ShapeDtypeStruct((1, NG), jnp.int32)),
        in_specs=[VM],
        out_specs=(VM, VM),
        scratch_shapes=[pltpu.VMEM((40, BUCKETS, 128), F32)],
        compiler_params=pltpu.CompilerParams(vmem_limit_bytes=20 * 2**20),
        cost_estimate=pl.CostEstimate(flops=10**9, bytes_accessed=10**6, transcendentals=0),
    )(key)


def densities(val, cond, cols, xs, k):
    for v in range(len(val)):
        vr, vi = val[v](cols)
        for c in range(2):
            cr = cond[c, 0, :, cols].astype(F32)
            ci = cond[c, 1, :, cols].astype(F32)
            rows = slice((v * 2 + c) * N, (v * 2 + c + 1) * N)
            xs[k, rows, 0:384] = (vr * cr + vi * ci).astype(BF16)
            xs[k, rows, 384:768] = (vr * ci - vi * cr).astype(BF16)


def sections(val, cond, wz, wy, xs, zs, s):
    count = zs.shape[1] // 2
    for i in range(6):
        densities(val, cond, slice(i * 384, (i + 1) * 384), xs, i % 2)
        out = jnp.dot(xs[i % 2], wz[...], preferred_element_type=F32).astype(BF16)
        for t in range(3):
            for f in range(2):
                zs[t, f * count : (f + 1) * count, i * 128 : (i + 1) * 128] = out[
                    :, f * 384 + t * 128 : f * 384 + (t + 1) * 128
                ]
    edge = lax.broadcasted_iota(jnp.int32, (1, 384), 1) % 24 == 0
    for t in range(3):
        cp = jnp.dot(zs[t], wy[:, :384], preferred_element_type=F32)
        sp = jnp.dot(zs[t], wy[:, 384:], preferred_element_type=F32)
        cre, cim, sre, sim = cp[:count], cp[count:], sp[:count], sp[count:]
        outs = (
            (jnp.where(edge, cre, cre + sim), jnp.where(edge, sre, cre - sim)),
            (jnp.where(edge, cim, cim - sre), jnp.where(edge, sim, cim + sre)),
        )
        for f in range(2):
            for e in range(2):
                cols = slice((t * 2 + e) * 384, (t * 2 + e + 1) * 384)
                s[f * count : (f + 1) * count, cols] = outs[f][e].astype(BF16)
    s[:, N * N :] = jnp.zeros((2 * count, WINDOW), BF16)


def select(s, tc, ts, starts, key, m, row):
    pairs = s.shape[0] // (2 * N)

    def step(group, _):
        todo = []
        keys = key[pl.ds(pl.multiple_of(group * 2 * GROUP, 8), 2 * GROUP), :]
        for u in range(GROUP):
            n = group * GROUP + u
            cols = pl.ds(pl.multiple_of(n * 256, 128), 256)
            waves = jnp.concatenate([keys[2 * u : 2 * u + 1], keys[2 * u + 1 : 2 * u + 2]], axis=1)
            column = waves >> 6
            kx = waves & 63
            hot = jnp.where(lax.broadcasted_iota(jnp.int32, (N, 256), 0) == kx, 1.0, 0.0).astype(BF16)
            co = jnp.dot(tc[...], hot, preferred_element_type=F32)
            si = jnp.dot(ts[...], hot, preferred_element_type=F32)
            low = starts[2 * n, 0] >> 13 << 7
            high = starts[2 * n + 1, 127] >> 6 | 127

            def window(base, column=column, co=co, si=si):
                rows = lax.broadcasted_iota(jnp.int32, (WINDOW, 256), 0)
                pick = jnp.where(rows == column - base, 1.0, 0.0).astype(BF16)
                part = s[:, pl.ds(pl.multiple_of(base, 128), WINDOW)]
                full = jnp.dot(part, pick, preferred_element_type=F32).reshape(2, pairs, N, 256)
                re = jnp.sum(full[0] * co + full[1] * si, axis=1)
                im = jnp.sum(full[1] * co - full[0] * si, axis=1)
                return re, im

            re, im = window(low)
            m[0, row : row + pairs, cols] = re
            m[1, row : row + pairs, cols] = im
            todo.append((window, low, high, cols))
        for window, low, high, cols in todo:

            def more(k, _, window=window, low=low, cols=cols):
                re, im = window(low + k * WINDOW)
                m[0, row : row + pairs, cols] += re
                m[1, row : row + pairs, cols] += im
                return 0

            lax.fori_loop(1, (high - low) // WINDOW + 1, more, 0)
        return 0

    lax.fori_loop(0, 20 // GROUP, step, 0)


def own_kernel(val, cond, wz, wy, tc, ts, starts, key, m, xs, zs, s):
    def band(cols):
        return val[0, 0, :, cols].astype(F32), val[0, 1, :, cols].astype(F32)

    sections([band], cond, wz, wy, xs, zs, s)
    select(s, tc, ts, starts, key, m, 0)


def rest_kernel(core, part, other, cond, wz, wy, tc, ts, starts, key, back, w, owned, left, right, xs, zs, s, m, mo):
    first = core[0] == 0

    def band(v):
        def read(cols):
            a = part[v, :, cols].astype(F32)
            b = other[v, :, cols].astype(F32)
            return jnp.where(first, a, b), jnp.where(first, b, a)

        return read

    sections([band(v) for v in range(3)], cond, wz, wy, xs, zs, s)
    select(s, tc, ts, starts, key, m, 2)
    m[:, 0:2, :] = owned[...]

    def unsort(group, _):
        for u in range(4):
            cols = pl.ds(pl.multiple_of((group * 4 + u) * 128, 128), 128)
            place = jnp.broadcast_to(back[:, cols], (8, 128))
            source = place >> 7
            lane = place & 127
            outs = [jnp.zeros((8, 128), F32)] * 2
            for k in range(40):
                hit = source == k
                for f in range(2):
                    got = jnp.take_along_axis(m[f, :, k * 128 : (k + 1) * 128], lane, axis=1)
                    outs[f] = jnp.where(hit, got, outs[f])
            for f in range(2):
                mo[f, :, cols] = outs[f]
        return 0

    lax.fori_loop(0, 10, unsort, 0)
    for z in range(8):
        for f in range(2):
            right[z, :, f * 640 : (f + 1) * 640] = mo[f, :, z * 640 : (z + 1) * 640].astype(BF16)
    weight = w[...]
    for r in range(16):
        parts = []
        for f in range(2):
            for b in range(4):
                lane = ((b // 2 * 4 + r // 4) * 2 + b % 2) * 320 + 80 * (r % 4)
                parts.append(mo[f, :, lane : lane + 80])
        left[r] = (weight * jnp.concatenate(parts, axis=1)).astype(BF16)


def scratch(pairs):
    rows = pairs * N
    return [
        pltpu.VMEM((2, rows, 768), BF16),
        pltpu.VMEM((3, 2 * rows, 768), BF16),
        pltpu.VMEM((2 * rows, N * N + WINDOW), BF16),
    ]


def own_coefficients(val, cond, wide, key):
    return pl.pallas_call(
        own_kernel,
        out_shape=jax.ShapeDtypeStruct((2, 2, NG), F32),
        in_specs=[VM] * 6 + [SM, VM],
        out_specs=VM,
        scratch_shapes=scratch(2),
        compiler_params=pltpu.CompilerParams(vmem_limit_bytes=40 * 2**20),
        cost_estimate=pl.CostEstimate(flops=5 * 10**9, bytes_accessed=3 * 10**7, transcendentals=0),
    )(val, cond, *wide, key, key)


def coefficients(core, part, other, cond, wide, key, back, w, owned):
    return pl.pallas_call(
        rest_kernel,
        out_shape=(
            jax.ShapeDtypeStruct((16, 8, 640), BF16),
            jax.ShapeDtypeStruct((8, 8, 1280), BF16),
        ),
        in_specs=[SM] + [VM] * 7 + [SM] + [VM] * 4,
        out_specs=(VM, VM),
        scratch_shapes=scratch(6) + [pltpu.VMEM((2, 8, NG), F32)] * 2,
        compiler_params=pltpu.CompilerParams(vmem_limit_bytes=40 * 2**20),
        cost_estimate=pl.CostEstimate(flops=10**10, bytes_accessed=5 * 10**7, transcendentals=0),
    )(core, part, other, cond, *wide, key, key, back, w, owned)


def chi_kernel(core, place, rows, l0, l1, l2, l3, r0, r1, r2, r3, mine, theirs, lall, lk, rk):
    for i, piece in enumerate((l0, l1, l2, l3)):
        lall[2 * i : 2 * i + 2] = piece[...]
    base = 0
    for piece in (r0, r1, r2, r3):
        size = piece.shape[0]
        rk[base : base + size] = piece[...]
        base += size

    def fill(k, _):
        r = rows[k]
        for u in range(4):
            pair = [lall[place[2 * u + e], r].astype(F32) for e in range(2)]
            lk[pl.ds(pl.multiple_of(k * 64 + u * 16, 16), 16), :] = jnp.concatenate(pair, axis=0).astype(BF16)
        return 0

    lax.fori_loop(0, 16, fill, 0)
    first = core[0] == 0
    half = 320

    def product(f):
        return lax.dot_general(
            lk[:, f * half : (f + 1) * half], rk[...], (((0,), (0,)), ((), ())), preferred_element_type=F32
        )

    re = product(0)
    im = product(1)
    chi_re = re[:, :640] + im[:, 640:]
    chi_im = im[:, :640] - re[:, 640:]
    for k, chi in enumerate((chi_re, chi_im)):
        a, b = chi[:, :half], chi[:, half:]
        cols = slice(k * half, (k + 1) * half)
        mine[:, cols] = jnp.where(first, a, b)
        theirs[:, cols] = jnp.where(first, b, a)


def chi_tiles(core, place, rows, lefts, rights):
    vm = pl.BlockSpec(memory_space=pltpu.VMEM)
    sm = pl.BlockSpec(memory_space=pltpu.SMEM)
    return pl.pallas_call(
        chi_kernel,
        out_shape=(jax.ShapeDtypeStruct((320, 640), F32),) * 2,
        in_specs=[sm] * 3 + [vm] * 8,
        out_specs=(vm, vm),
        scratch_shapes=[
            pltpu.VMEM((8, 16, 8, 640), BF16),
            pltpu.VMEM((1024, 640), BF16),
            pltpu.VMEM((1024, 1280), BF16),
        ],
        compiler_params=pltpu.CompilerParams(vmem_limit_bytes=48 * 2**20),
    )(core, place, rows, *lefts, *rights)


def send(values, target):
    def index(z, y, x, c):
        return ((((z % 4) * 4 + y % 4) * 4 + x % 4) * 2 + (z % 8) // 4) * 2 + c

    pairs = [
        (index(z, y, x, c), index(*target(z, y, x, c)))
        for z in range(8)
        for y in range(4)
        for x in range(4)
        for c in range(2)
    ]
    return lax.ppermute(values, AXES, pairs)


def send_z(values, step):
    return send(values, lambda z, y, x, c: (z + step, y, x, c))


def send_core(values):
    return send(values, lambda z, y, x, c: (z, y, x, 1 - c))


def plane(axis, move):
    def target(z, y, x, c):
        if axis == c:
            return z, y, move(x), c
        return z, move(y), x, c

    return target


def outward(a):
    return a + 1 if a % 2 else a - 1


def inward(a):
    return a ^ 1


def ring(move):
    def target(z, y, x, c):
        return (move((z - c) % 8) + c) % 8, y, x, c

    return target


def assemble_kernel(tile, re, im):
    for f, out in enumerate((re, im)):
        parts = [tile[k, :, f * 320 : (f + 1) * 320].astype(F32) for k in range(4)]
        out[...] = jnp.concatenate(parts, axis=1)


def assemble(tile):
    return pl.pallas_call(
        assemble_kernel,
        out_shape=(jax.ShapeDtypeStruct((80, 1280), F32),) * 2,
        in_specs=[VM],
        out_specs=(VM, VM),
    )(tile)


def local(valence, conduction, valence_energy, conduction_energy, g_index):
    p, y, x, h, c = (lax.axis_index(a) for a in AXES)
    z = h * 4 + p
    core = jnp.reshape(c, (1,)).astype(jnp.int32)

    piece = lax.dynamic_index_in_dim(valence[0], c, 0, keepdims=False)
    part = jnp.concatenate(
        [
            send_z(piece, -1)[None],
            jnp.concatenate([send_z(piece[:32], 2), send_z(piece[32:], -2)])[None],
            send_z(piece, 1)[None],
        ]
    )
    other = send_core(part)

    order = g_index.reshape(2, 2, 4, 320).transpose(0, 2, 1, 3).reshape(NG)
    plane_part = lax.rem(order, N * N)
    key = (column_of(lax.div(plane_part, N), lax.rem(plane_part, N)) << 6) | lax.div(order, N * N)
    key, back = sort_waves(key.reshape(1, NG))

    energies = lax.dynamic_slice(jnp.tile(valence_energy, 2), (p,), (NV,))
    scale = math.sqrt(NV * 512)
    weight = 2.0 / ((energies[:, None] - conduction_energy[None, :]) * scale)

    wide = [jnp.asarray(t) for t in wide_tables()]
    owned = own_coefficients(valence, conduction, wide, key)
    left, right = coefficients(
        core, part, other, conduction, wide, key, back, weight.reshape(8, 1), owned
    )

    right = lax.all_to_all(right, ("h", "p"), 0, 0, tiled=True).reshape(64, 1280)
    left, right = lax.optimization_barrier((left, right))
    left = lax.all_to_all(left, ("y", "x"), 0, 0, tiled=True)
    zz = (z - c) % 8
    left0 = jnp.stack([left, send(left, ring(inward))])
    left1 = send(left0, ring(outward))
    left2 = send(left1, ring(inward))
    left3 = send(left2, ring(outward))
    near = zz ^ 1
    one = (zz + 2 * (zz % 2) - 1) % 8
    two = (near + 2 * (near % 2) - 1) % 8
    three = ((one ^ 1) + 2 * ((one ^ 1) % 2) - 1) % 8
    held = jnp.stack([zz, near, one, one ^ 1, two, two ^ 1, three, three ^ 1])
    held = (held + c) % 8
    place = jnp.argmax(held[None, :] == jnp.arange(8)[:, None], axis=1).astype(jnp.int32)

    moves = (lambda i: i + 1, lambda i: i - 1, lambda i: i + 2)
    offsets = jnp.array([0, 3, 1, 2])
    four = jnp.concatenate([right] + [send(right, plane(0, move)) for move in moves])
    rights = [four] + [send(four, plane(1, move)) for move in moves]
    aa = jnp.tile((jnp.where(c == 0, x, y) + offsets) % 4, 4)
    bb = jnp.repeat((jnp.where(c == 0, y, x) + offsets) % 4, 4)
    rows = jnp.where(c == 0, bb * 4 + aa, aa * 4 + bb).astype(jnp.int32)

    mine, theirs = chi_tiles(core, place, rows, (left0, left1, left2, left3), rights)
    tile = (mine + send_core(theirs)).astype(BF16).reshape(4, 80, 640)
    return assemble(lax.all_to_all(tile, "p", 0, 0, tiled=True))


def solution(mesh):
    fine = Mesh(mesh.devices.reshape(4, 4, 4, 2, 2), AXES)
    bands = P(AXES)
    return jax.shard_map(
        local,
        mesh=fine,
        in_specs=(P("p"), bands, P(), bands, P()),
        out_specs=(P(("p", "y", "x"), ("h", "c")),) * 2,
        check_vma=False,
    )
```

```python
import functools
import math

import jax
import jax.numpy as jnp
import ml_dtypes
import numpy as np
from jax import lax
from jax.experimental import pallas as pl
from jax.experimental.pallas import tpu as pltpu
from jax.sharding import Mesh, PartitionSpec as P

NV = 4
N = 48
NG = 5120
F32 = jnp.float32
BF16 = jnp.bfloat16
WINDOW = 256
GROUP = 4
BUCKETS = 24
VM = pl.BlockSpec(memory_space=pltpu.VMEM)
SM = pl.BlockSpec(memory_space=pltpu.SMEM)
AXES = ("p", "y", "x", "h", "c")


def tables():
    k = np.arange(N)
    ang = (k[:, None] * k[None, :] % N).astype(np.float32) * np.float32(2.0 * math.pi / N)
    fac = np.float32(1.0 / math.sqrt(N))
    cos = (np.cos(ang) * fac).astype(ml_dtypes.bfloat16)
    sin = (np.sin(ang) * fac).astype(ml_dtypes.bfloat16)
    return cos, sin


def wide_tables():
    cos, sin = tables()
    cs = cos.astype(np.float32)
    sn = sin.astype(np.float32)
    eye8 = np.eye(8, dtype=np.float32)
    wz = np.zeros((2, 8, 48, 2, 48, 8), np.float32)
    for (f, g, tab) in ((0, 0, cs), (1, 0, sn), (0, 1, -sn), (1, 1, cs)):
        wz[f, :, :, g] = np.einsum("ab,kz->azkb", eye8, tab)
    wz = wz.reshape(768, 768)
    eye16 = np.eye(16, dtype=np.float32)
    wy = np.zeros((6, 16, 8, 2, 16, 24), np.float32)
    half = sn[:24].copy()
    half[0] = cs[24]
    for j, tab in enumerate((cs[:24], half)):
        wy[:, :, :, j] = np.einsum("ab,kmi->maibk", eye16, tab.reshape(24, 6, 8))
    wy = wy.reshape(768, 768)
    return wz.astype(ml_dtypes.bfloat16), wy.astype(ml_dtypes.bfloat16), cos, sin


def column_of(y, z):
    within = jnp.where(y < 24, y, jnp.where(y == 24, 0, N - y))
    return (z >> 4) * 768 + jnp.where(y < 24, 0, 384) + (z & 15) * 24 + within


def sort_kernel(key, keys, place, held):
    bucket = key[...] >> 13
    slots = lax.broadcasted_iota(jnp.int32, (BUCKETS, 128), 0)
    before = jnp.zeros((BUCKETS, 128), F32)
    for k in range(40):
        mine = bucket[:, k * 128 : (k + 1) * 128]
        held[k] = jnp.where(slots == mine, 1.0, 0.0)
        before += jnp.where(mine < slots, 1.0, 0.0)
    upto = lax.broadcasted_iota(jnp.int32, (128, 128), 0) <= lax.broadcasted_iota(jnp.int32, (128, 128), 1)
    counts = jnp.dot(
        held[...].reshape(40 * BUCKETS, 128).astype(BF16),
        jnp.where(upto, 1.0, 0.0).astype(BF16),
        preferred_element_type=F32,
    ).reshape(40, BUCKETS, 128)
    base = jnp.sum(before, axis=1, keepdims=True) - 1.0
    for k in range(40):
        rank = jnp.sum(held[k] * (base + counts[k]), axis=0, keepdims=True)
        place[:, k * 128 : (k + 1) * 128] = rank.astype(jnp.int32)
        base = base + counts[k, :, 127:128]
    high = place[...] >> 7
    low = place[...] & 127
    at = lax.broadcasted_iota(jnp.int32, (40, NG), 0) == high
    parts = (bucket, (key[...] >> 6) & 127, key[...] & 63)
    rows = jnp.concatenate([jnp.where(at, v.astype(F32), 0.0) for v in parts], axis=0).astype(BF16)
    cols = jnp.where(lax.broadcasted_iota(jnp.int32, (128, NG), 0) == low, 1.0, 0.0).astype(BF16)
    moved = lax.dot_general(rows, cols, (((1,), (1,)), ((), ())), preferred_element_type=F32).astype(jnp.int32)
    keys[...] = (moved[0:40] << 13) | (moved[40:80] << 6) | moved[80:120]


def sort_waves(key):
    return pl.pallas_call(
        sort_kernel,
        out_shape=(jax.ShapeDtypeStruct((40, 128), jnp.int32), jax.ShapeDtypeStruct((1, NG), jnp.int32)),
        in_specs=[VM],
        out_specs=(VM, VM),
        scratch_shapes=[pltpu.VMEM((40, BUCKETS, 128), F32)],
        compiler_params=pltpu.CompilerParams(vmem_limit_bytes=20 * 2**20),
        cost_estimate=pl.CostEstimate(flops=10**9, bytes_accessed=10**6, transcendentals=0),
    )(key)


def densities(val, cond, cols, xs, k):
    for v in range(len(val)):
        vr, vi = val[v](cols)
        for c in range(2):
            cr = cond[c, 0, :, cols].astype(F32)
            ci = cond[c, 1, :, cols].astype(F32)
            rows = slice((v * 2 + c) * N, (v * 2 + c + 1) * N)
            xs[k, rows, 0:384] = (vr * cr + vi * ci).astype(BF16)
            xs[k, rows, 384:768] = (vr * ci - vi * cr).astype(BF16)


def sections(val, cond, wz, wy, xs, zs, s):
    count = zs.shape[1] // 2
    for i in range(6):
        densities(val, cond, slice(i * 384, (i + 1) * 384), xs, i % 2)
        out = jnp.dot(xs[i % 2], wz[...], preferred_element_type=F32).astype(BF16)
        for t in range(3):
            for f in range(2):
                zs[t, f * count : (f + 1) * count, i * 128 : (i + 1) * 128] = out[
                    :, f * 384 + t * 128 : f * 384 + (t + 1) * 128
                ]
    edge = lax.broadcasted_iota(jnp.int32, (1, 384), 1) % 24 == 0
    for t in range(3):
        cp = jnp.dot(zs[t], wy[:, :384], preferred_element_type=F32)
        sp = jnp.dot(zs[t], wy[:, 384:], preferred_element_type=F32)
        cre, cim, sre, sim = cp[:count], cp[count:], sp[:count], sp[count:]
        outs = (
            (jnp.where(edge, cre, cre + sim), jnp.where(edge, sre, cre - sim)),
            (jnp.where(edge, cim, cim - sre), jnp.where(edge, sim, cim + sre)),
        )
        for f in range(2):
            for e in range(2):
                cols = slice((t * 2 + e) * 384, (t * 2 + e + 1) * 384)
                s[f * count : (f + 1) * count, cols] = outs[f][e].astype(BF16)
    s[:, N * N :] = jnp.zeros((2 * count, WINDOW), BF16)


def select(s, tc, ts, starts, key, m, row):
    pairs = s.shape[0] // (2 * N)

    def step(group, _):
        todo = []
        keys = key[pl.ds(pl.multiple_of(group * 2 * GROUP, 8), 2 * GROUP), :]
        for u in range(GROUP):
            n = group * GROUP + u
            cols = pl.ds(pl.multiple_of(n * 256, 128), 256)
            waves = jnp.concatenate([keys[2 * u : 2 * u + 1], keys[2 * u + 1 : 2 * u + 2]], axis=1)
            column = waves >> 6
            kx = waves & 63
            hot = jnp.where(lax.broadcasted_iota(jnp.int32, (N, 256), 0) == kx, 1.0, 0.0).astype(BF16)
            co = jnp.dot(tc[...], hot, preferred_element_type=F32)
            si = jnp.dot(ts[...], hot, preferred_element_type=F32)
            low = starts[2 * n, 0] >> 13 << 7
            high = starts[2 * n + 1, 127] >> 6 | 127

            def window(base, column=column, co=co, si=si):
                rows = lax.broadcasted_iota(jnp.int32, (WINDOW, 256), 0)
                pick = jnp.where(rows == column - base, 1.0, 0.0).astype(BF16)
                part = s[:, pl.ds(pl.multiple_of(base, 128), WINDOW)]
                full = jnp.dot(part, pick, preferred_element_type=F32).reshape(2, pairs, N, 256)
                re = jnp.sum(full[0] * co + full[1] * si, axis=1)
                im = jnp.sum(full[1] * co - full[0] * si, axis=1)
                return re, im

            re, im = window(low)
            m[0, row : row + pairs, cols] = re
            m[1, row : row + pairs, cols] = im
            todo.append((window, low, high, cols))
        for window, low, high, cols in todo:

            def more(k, _, window=window, low=low, cols=cols):
                re, im = window(low + k * WINDOW)
                m[0, row : row + pairs, cols] += re
                m[1, row : row + pairs, cols] += im
                return 0

            lax.fori_loop(1, (high - low) // WINDOW + 1, more, 0)
        return 0

    lax.fori_loop(0, 20 // GROUP, step, 0)


def own_kernel(val, cond, wz, wy, tc, ts, starts, key, m, xs, zs, s):
    def band(cols):
        return val[0, 0, :, cols].astype(F32), val[0, 1, :, cols].astype(F32)

    sections([band], cond, wz, wy, xs, zs, s)
    select(s, tc, ts, starts, key, m, 0)


def rest_kernel(core, part, other, cond, wz, wy, tc, ts, starts, key, back, w, owned, left, right, xs, zs, s, m, mo):
    first = core[0] == 0

    def band(v):
        def read(cols):
            a = part[v, :, cols].astype(F32)
            b = other[v, :, cols].astype(F32)
            return jnp.where(first, a, b), jnp.where(first, b, a)

        return read

    sections([band(v) for v in range(3)], cond, wz, wy, xs, zs, s)
    select(s, tc, ts, starts, key, m, 2)
    m[:, 0:2, :] = owned[...]

    def unsort(group, _):
        for u in range(4):
            cols = pl.ds(pl.multiple_of((group * 4 + u) * 128, 128), 128)
            place = jnp.broadcast_to(back[:, cols], (8, 128))
            source = place >> 7
            lane = place & 127
            outs = [jnp.zeros((8, 128), F32)] * 2
            for k in range(40):
                hit = source == k
                for f in range(2):
                    got = jnp.take_along_axis(m[f, :, k * 128 : (k + 1) * 128], lane, axis=1)
                    outs[f] = jnp.where(hit, got, outs[f])
            for f in range(2):
                mo[f, :, cols] = outs[f]
        return 0

    lax.fori_loop(0, 10, unsort, 0)
    for z in range(8):
        for f in range(2):
            right[z, :, f * 640 : (f + 1) * 640] = mo[f, :, z * 640 : (z + 1) * 640].astype(BF16)
    weight = w[...]
    for r in range(16):
        parts = []
        for f in range(2):
            for b in range(4):
                lane = ((b // 2 * 4 + r // 4) * 2 + b % 2) * 320 + 80 * (r % 4)
                parts.append(mo[f, :, lane : lane + 80])
        left[r] = (weight * jnp.concatenate(parts, axis=1)).astype(BF16)


def scratch(pairs):
    rows = pairs * N
    return [
        pltpu.VMEM((2, rows, 768), BF16),
        pltpu.VMEM((3, 2 * rows, 768), BF16),
        pltpu.VMEM((2 * rows, N * N + WINDOW), BF16),
    ]


def own_coefficients(val, cond, wide, key):
    return pl.pallas_call(
        own_kernel,
        out_shape=jax.ShapeDtypeStruct((2, 2, NG), F32),
        in_specs=[VM] * 6 + [SM, VM],
        out_specs=VM,
        scratch_shapes=scratch(2),
        compiler_params=pltpu.CompilerParams(vmem_limit_bytes=40 * 2**20),
        cost_estimate=pl.CostEstimate(flops=5 * 10**9, bytes_accessed=3 * 10**7, transcendentals=0),
    )(val, cond, *wide, key, key)


def coefficients(core, part, other, cond, wide, key, back, w, owned):
    return pl.pallas_call(
        rest_kernel,
        out_shape=(
            jax.ShapeDtypeStruct((16, 8, 640), BF16),
            jax.ShapeDtypeStruct((8, 8, 1280), BF16),
        ),
        in_specs=[SM] + [VM] * 7 + [SM] + [VM] * 4,
        out_specs=(VM, VM),
        scratch_shapes=scratch(6) + [pltpu.VMEM((2, 8, NG), F32)] * 2,
        compiler_params=pltpu.CompilerParams(vmem_limit_bytes=40 * 2**20),
        cost_estimate=pl.CostEstimate(flops=10**10, bytes_accessed=5 * 10**7, transcendentals=0),
    )(core, part, other, cond, *wide, key, key, back, w, owned)


def chi_kernel(core, place, rows, l0, l1, l2, l3, r0, r1, r2, r3, mine, theirs, lall, lk, rk):
    for i, piece in enumerate((l0, l1, l2, l3)):
        lall[2 * i : 2 * i + 2] = piece[...]
    base = 0
    for piece in (r0, r1, r2, r3):
        size = piece.shape[0]
        rk[base : base + size] = piece[...]
        base += size

    def fill(k, _):
        r = rows[k]
        for u in range(4):
            pair = [lall[place[2 * u + e], r].astype(F32) for e in range(2)]
            lk[pl.ds(pl.multiple_of(k * 64 + u * 16, 16), 16), :] = jnp.concatenate(pair, axis=0).astype(BF16)
        return 0

    lax.fori_loop(0, 16, fill, 0)
    first = core[0] == 0
    half = 320

    def product(f):
        return lax.dot_general(
            lk[:, f * half : (f + 1) * half], rk[...], (((0,), (0,)), ((), ())), preferred_element_type=F32
        )

    re = product(0)
    im = product(1)
    chi_re = re[:, :640] + im[:, 640:]
    chi_im = im[:, :640] - re[:, 640:]
    for k, chi in enumerate((chi_re, chi_im)):
        a, b = chi[:, :half], chi[:, half:]
        cols = slice(k * half, (k + 1) * half)
        mine[:, cols] = jnp.where(first, a, b)
        theirs[:, cols] = jnp.where(first, b, a)


def chi_tiles(core, place, rows, lefts, rights):
    vm = pl.BlockSpec(memory_space=pltpu.VMEM)
    sm = pl.BlockSpec(memory_space=pltpu.SMEM)
    return pl.pallas_call(
        chi_kernel,
        out_shape=(jax.ShapeDtypeStruct((320, 640), F32),) * 2,
        in_specs=[sm] * 3 + [vm] * 8,
        out_specs=(vm, vm),
        scratch_shapes=[
            pltpu.VMEM((8, 16, 8, 640), BF16),
            pltpu.VMEM((1024, 640), BF16),
            pltpu.VMEM((1024, 1280), BF16),
        ],
        compiler_params=pltpu.CompilerParams(vmem_limit_bytes=48 * 2**20),
    )(core, place, rows, *lefts, *rights)


def device(z, y, x, c):
    return ((((z % 4) * 4 + y % 4) * 4 + x % 4) * 2 + (z % 8) // 4) * 2 + c


def send(values, target):
    pairs = [
        (device(z, y, x, c), device(*target(z, y, x, c)))
        for z in range(8)
        for y in range(4)
        for x in range(4)
        for c in range(2)
    ]
    return lax.ppermute(values, AXES, pairs)


def send_z(values, step):
    return send(values, lambda z, y, x, c: (z + step, y, x, c))


def send_core(values):
    return send(values, lambda z, y, x, c: (z, y, x, 1 - c))


def plane(axis, move):
    def target(z, y, x, c):
        if axis == c:
            return z, y, move(x), c
        return z, move(y), x, c

    return target


def outward(a):
    return a + 1 if a % 2 else a - 1


def inward(a):
    return a ^ 1


def ring(move):
    def target(z, y, x, c):
        return (move((z - c) % 8) + c) % 8, y, x, c

    return target


def pair_exchange(left):
    groups = []
    for c in range(2):
        for k in range(4):
            zs = [(2 * k + e + c) % 8 for e in range(2)]
            groups.append([device(z, y, x, c) for z in zs for y in range(4) for x in range(4)])
    twice = jnp.concatenate([left, left])
    got = lax.all_to_all(twice, AXES, 0, 0, axis_index_groups=groups, tiled=True)
    return got.reshape(2, 16, 8, 640)


def assemble_kernel(tile, re, im):
    for f, out in enumerate((re, im)):
        parts = [tile[k, :, f * 320 : (f + 1) * 320].astype(F32) for k in range(4)]
        out[...] = jnp.concatenate(parts, axis=1)


def assemble(tile):
    return pl.pallas_call(
        assemble_kernel,
        out_shape=(jax.ShapeDtypeStruct((80, 1280), F32),) * 2,
        in_specs=[VM],
        out_specs=(VM, VM),
    )(tile)


def local(valence, conduction, valence_energy, conduction_energy, g_index):
    p, y, x, h, c = (lax.axis_index(a) for a in AXES)
    z = h * 4 + p
    core = jnp.reshape(c, (1,)).astype(jnp.int32)

    piece = lax.dynamic_index_in_dim(valence[0], c, 0, keepdims=False)
    part = jnp.concatenate(
        [
            send_z(piece, -1)[None],
            send(piece, lambda z, y, x, c: (z + 2 - 4 * c, y, x, c))[None],
            send_z(piece, 1)[None],
        ]
    )

    order = g_index.reshape(2, 2, 4, 320).transpose(0, 2, 1, 3).reshape(NG)
    plane_part = lax.rem(order, N * N)
    key = (column_of(lax.div(plane_part, N), lax.rem(plane_part, N)) << 6) | lax.div(order, N * N)
    key, back = sort_waves(key.reshape(1, NG))

    energies = lax.dynamic_slice(jnp.tile(valence_energy, 2), (p,), (NV,))
    scale = math.sqrt(NV * 512)
    weight = 2.0 / ((energies[:, None] - conduction_energy[None, :]) * scale)

    wide = [jnp.asarray(t) for t in wide_tables()]
    owned = own_coefficients(valence, conduction, wide, key)
    part, owned = lax.optimization_barrier((part, owned))
    other = send_core(part)
    left, right = coefficients(
        core, part, other, conduction, wide, key, back, weight.reshape(8, 1), owned
    )

    right = lax.all_to_all(right, ("h", "p"), 0, 0, tiled=True).reshape(64, 1280)
    left, right = lax.optimization_barrier((left, right))
    left0 = pair_exchange(left)
    zz = (z - c) % 8
    left1 = send(left0, ring(outward))
    left2 = send(left1, ring(inward))
    left3 = send(left2, ring(outward))
    near = zz ^ 1
    one = (zz + 2 * (zz % 2) - 1) % 8
    two = (near + 2 * (near % 2) - 1) % 8
    three = ((one ^ 1) + 2 * ((one ^ 1) % 2) - 1) % 8
    held = jnp.stack([zz & 6, zz | 1, one & 6, one | 1, two & 6, two | 1, three & 6, three | 1])
    held = (held + c) % 8
    place = jnp.argmax(held[None, :] == jnp.arange(8)[:, None], axis=1).astype(jnp.int32)

    moves = (lambda i: i + 1, lambda i: i - 1, lambda i: i + 2)
    offsets = jnp.array([0, 3, 1, 2])
    four = jnp.concatenate([right] + [send(right, plane(0, move)) for move in moves])
    rights = [four] + [send(four, plane(1, move)) for move in moves]
    aa = jnp.tile((jnp.where(c == 0, x, y) + offsets) % 4, 4)
    bb = jnp.repeat((jnp.where(c == 0, y, x) + offsets) % 4, 4)
    rows = jnp.where(c == 0, bb * 4 + aa, aa * 4 + bb).astype(jnp.int32)

    mine, theirs = chi_tiles(core, place, rows, (left0, left1, left2, left3), rights)
    tile = (mine + send_core(theirs)).astype(BF16).reshape(4, 80, 640)
    return assemble(lax.all_to_all(tile, "p", 0, 0, tiled=True))


def solution(mesh):
    fine = Mesh(mesh.devices.reshape(4, 4, 4, 2, 2), AXES)
    bands = P(AXES)
    return jax.shard_map(
        local,
        mesh=fine,
        in_specs=(P("p"), bands, P(), bands, P()),
        out_specs=(P(("p", "y", "x"), ("h", "c")),) * 2,
        check_vma=False,
    )
```

```python
import functools
import math

import jax
import jax.numpy as jnp
import ml_dtypes
import numpy as np
from jax import lax
from jax.experimental import pallas as pl
from jax.experimental.pallas import tpu as pltpu
from jax.sharding import Mesh, PartitionSpec as P

NV = 4
N = 48
NG = 5120
F32 = jnp.float32
BF16 = jnp.bfloat16
WINDOW = 256
GROUP = 4
BUCKETS = 24
VM = pl.BlockSpec(memory_space=pltpu.VMEM)
SM = pl.BlockSpec(memory_space=pltpu.SMEM)
AXES = ("p", "y", "x", "h", "c")


def tables():
    k = np.arange(N)
    ang = (k[:, None] * k[None, :] % N).astype(np.float32) * np.float32(2.0 * math.pi / N)
    fac = np.float32(1.0 / math.sqrt(N))
    cos = (np.cos(ang) * fac).astype(ml_dtypes.bfloat16)
    sin = (np.sin(ang) * fac).astype(ml_dtypes.bfloat16)
    return cos, sin


def wide_tables():
    cos, sin = tables()
    cs = cos.astype(np.float32)
    sn = sin.astype(np.float32)
    eye8 = np.eye(8, dtype=np.float32)
    wz = np.zeros((2, 8, 48, 2, 48, 8), np.float32)
    for (f, g, tab) in ((0, 0, cs), (1, 0, sn), (0, 1, -sn), (1, 1, cs)):
        wz[f, :, :, g] = np.einsum("ab,kz->azkb", eye8, tab)
    wz = wz.reshape(768, 768)
    eye16 = np.eye(16, dtype=np.float32)
    wy = np.zeros((6, 16, 8, 2, 16, 24), np.float32)
    half = sn[:24].copy()
    half[0] = cs[24]
    for j, tab in enumerate((cs[:24], half)):
        wy[:, :, :, j] = np.einsum("ab,kmi->maibk", eye16, tab.reshape(24, 6, 8))
    wy = wy.reshape(768, 768)
    return np.stack([wz, wy]).astype(ml_dtypes.bfloat16), cos, sin


def column_of(y, z):
    within = jnp.where(y < 24, y, jnp.where(y == 24, 0, N - y))
    return (z >> 4) * 768 + jnp.where(y < 24, 0, 384) + (z & 15) * 24 + within


def wave_keys(waves):
    x = ((waves.astype(F32) + 0.5) * (1.0 / (N * N))).astype(jnp.int32)
    rest = waves - x * (N * N)
    y = ((rest.astype(F32) + 0.5) * (1.0 / N)).astype(jnp.int32)
    key = (column_of(y, rest - y * N) << 6) | x
    starts = [(2 * h + c) * 1280 + p * 320 for h in range(2) for p in range(4) for c in range(2)]
    return jnp.concatenate([key[:, s : s + 320] for s in starts], axis=1)


def sort_kernel(waves, keys, place, held):
    key = wave_keys(waves[...])
    bucket = key >> 13
    slots = lax.broadcasted_iota(jnp.int32, (BUCKETS, 128), 0)
    before = jnp.zeros((BUCKETS, 128), F32)
    for k in range(40):
        mine = bucket[:, k * 128 : (k + 1) * 128]
        held[k] = jnp.where(slots == mine, 1.0, 0.0)
        before += jnp.where(mine < slots, 1.0, 0.0)
    upto = lax.broadcasted_iota(jnp.int32, (128, 128), 0) <= lax.broadcasted_iota(jnp.int32, (128, 128), 1)
    counts = jnp.dot(
        held[...].reshape(40 * BUCKETS, 128).astype(BF16),
        jnp.where(upto, 1.0, 0.0).astype(BF16),
        preferred_element_type=F32,
    ).reshape(40, BUCKETS, 128)
    base = jnp.sum(before, axis=1, keepdims=True) - 1.0
    for k in range(40):
        rank = jnp.sum(held[k] * (base + counts[k]), axis=0, keepdims=True)
        place[:, k * 128 : (k + 1) * 128] = rank.astype(jnp.int32)
        base = base + counts[k, :, 127:128]
    high = place[...] >> 7
    low = place[...] & 127
    at = lax.broadcasted_iota(jnp.int32, (40, NG), 0) == high
    parts = (bucket, (key >> 6) & 127, key & 63)
    rows = jnp.concatenate([jnp.where(at, v.astype(F32), 0.0) for v in parts], axis=0).astype(BF16)
    cols = jnp.where(lax.broadcasted_iota(jnp.int32, (128, NG), 0) == low, 1.0, 0.0).astype(BF16)
    moved = lax.dot_general(rows, cols, (((1,), (1,)), ((), ())), preferred_element_type=F32).astype(jnp.int32)
    keys[...] = (moved[0:40] << 13) | (moved[40:80] << 6) | moved[80:120]


def sort_waves(waves):
    return pl.pallas_call(
        sort_kernel,
        out_shape=(jax.ShapeDtypeStruct((40, 128), jnp.int32), jax.ShapeDtypeStruct((1, NG), jnp.int32)),
        in_specs=[VM],
        out_specs=(VM, VM),
        scratch_shapes=[pltpu.VMEM((40, BUCKETS, 128), F32)],
        compiler_params=pltpu.CompilerParams(vmem_limit_bytes=20 * 2**20),
        cost_estimate=pl.CostEstimate(flops=10**9, bytes_accessed=10**6, transcendentals=0),
    )(waves)


def densities(val, cond, cols, xs, k):
    for v in range(len(val)):
        vr, vi = val[v](cols)
        for c in range(2):
            cr = cond[c, 0, :, cols].astype(F32)
            ci = cond[c, 1, :, cols].astype(F32)
            rows = slice((v * 2 + c) * N, (v * 2 + c + 1) * N)
            xs[k, rows, 0:384] = (vr * cr + vi * ci).astype(BF16)
            xs[k, rows, 384:768] = (vr * ci - vi * cr).astype(BF16)


def sections(val, cond, wide, xs, zs, s):
    count = zs.shape[1] // 2
    for i in range(6):
        densities(val, cond, slice(i * 384, (i + 1) * 384), xs, i % 2)
        out = jnp.dot(xs[i % 2], wide[0], preferred_element_type=F32).astype(BF16)
        for t in range(3):
            for f in range(2):
                zs[t, f * count : (f + 1) * count, i * 128 : (i + 1) * 128] = out[
                    :, f * 384 + t * 128 : f * 384 + (t + 1) * 128
                ]
    edge = lax.broadcasted_iota(jnp.int32, (1, 384), 1) % 24 == 0
    for t in range(3):
        cp = jnp.dot(zs[t], wide[1, :, :384], preferred_element_type=F32)
        sp = jnp.dot(zs[t], wide[1, :, 384:], preferred_element_type=F32)
        cre, cim, sre, sim = cp[:count], cp[count:], sp[:count], sp[count:]
        outs = (
            (jnp.where(edge, cre, cre + sim), jnp.where(edge, sre, cre - sim)),
            (jnp.where(edge, cim, cim - sre), jnp.where(edge, sim, cim + sre)),
        )
        for f in range(2):
            for e in range(2):
                cols = slice((t * 2 + e) * 384, (t * 2 + e + 1) * 384)
                s[f * count : (f + 1) * count, cols] = outs[f][e].astype(BF16)
    s[:, N * N :] = jnp.zeros((2 * count, WINDOW), BF16)


def select(s, tc, ts, starts, key, m, row):
    pairs = s.shape[0] // (2 * N)

    def step(group, _):
        todo = []
        keys = key[pl.ds(pl.multiple_of(group * 2 * GROUP, 8), 2 * GROUP), :]
        for u in range(GROUP):
            n = group * GROUP + u
            cols = pl.ds(pl.multiple_of(n * 256, 128), 256)
            waves = jnp.concatenate([keys[2 * u : 2 * u + 1], keys[2 * u + 1 : 2 * u + 2]], axis=1)
            column = waves >> 6
            kx = waves & 63
            hot = jnp.where(lax.broadcasted_iota(jnp.int32, (N, 256), 0) == kx, 1.0, 0.0).astype(BF16)
            co = jnp.dot(tc[...], hot, preferred_element_type=F32)
            si = jnp.dot(ts[...], hot, preferred_element_type=F32)
            low = starts[2 * n, 0] >> 13 << 7
            high = starts[2 * n + 1, 127] >> 6 | 127

            def window(base, column=column, co=co, si=si):
                rows = lax.broadcasted_iota(jnp.int32, (WINDOW, 256), 0)
                pick = jnp.where(rows == column - base, 1.0, 0.0).astype(BF16)
                part = s[:, pl.ds(pl.multiple_of(base, 128), WINDOW)]
                full = jnp.dot(part, pick, preferred_element_type=F32).reshape(2, pairs, N, 256)
                re = jnp.sum(full[0] * co + full[1] * si, axis=1)
                im = jnp.sum(full[1] * co - full[0] * si, axis=1)
                return re, im

            re, im = window(low)
            m[0, row : row + pairs, cols] = re
            m[1, row : row + pairs, cols] = im
            todo.append((window, low, high, cols))
        for window, low, high, cols in todo:

            def more(k, _, window=window, low=low, cols=cols):
                re, im = window(low + k * WINDOW)
                m[0, row : row + pairs, cols] += re
                m[1, row : row + pairs, cols] += im
                return 0

            lax.fori_loop(1, (high - low) // WINDOW + 1, more, 0)
        return 0

    lax.fori_loop(0, 20 // GROUP, step, 0)


def own_kernel(val, cond, wide, tc, ts, starts, key, m, xs, zs, s):
    def band(cols):
        return val[0, 0, :, cols].astype(F32), val[0, 1, :, cols].astype(F32)

    sections([band], cond, wide, xs, zs, s)
    select(s, tc, ts, starts, key, m, 0)


def rest_kernel(core, part, other, cond, wide, tc, ts, starts, key, back, w, owned, left, right, xs, zs, s, m, mo):
    first = core[0] == 0

    def band(v):
        def read(cols):
            a = part[v, :, cols].astype(F32)
            b = other[v, :, cols].astype(F32)
            return jnp.where(first, a, b), jnp.where(first, b, a)

        return read

    sections([band(v) for v in range(3)], cond, wide, xs, zs, s)
    select(s, tc, ts, starts, key, m, 2)
    m[:, 0:2, :] = owned[...]

    def unsort(group, _):
        for u in range(4):
            cols = pl.ds(pl.multiple_of((group * 4 + u) * 128, 128), 128)
            place = jnp.broadcast_to(back[:, cols], (8, 128))
            source = place >> 7
            lane = place & 127
            outs = [jnp.zeros((8, 128), F32)] * 2
            for k in range(40):
                hit = source == k
                for f in range(2):
                    got = jnp.take_along_axis(m[f, :, k * 128 : (k + 1) * 128], lane, axis=1)
                    outs[f] = jnp.where(hit, got, outs[f])
            for f in range(2):
                mo[f, :, cols] = outs[f]
        return 0

    lax.fori_loop(0, 10, unsort, 0)
    for z in range(8):
        for f in range(2):
            right[z, :, f * 640 : (f + 1) * 640] = mo[f, :, z * 640 : (z + 1) * 640].astype(BF16)
    weight = w[...]
    for r in range(16):
        parts = []
        for f in range(2):
            for b in range(4):
                lane = ((b // 2 * 4 + r // 4) * 2 + b % 2) * 320 + 80 * (r % 4)
                parts.append(mo[f, :, lane : lane + 80])
        block = (weight * jnp.concatenate(parts, axis=1)).astype(BF16)
        left[r] = block
        left[16 + r] = block


def scratch(pairs):
    rows = pairs * N
    return [
        pltpu.VMEM((2, rows, 768), BF16),
        pltpu.VMEM((3, 2 * rows, 768), BF16),
        pltpu.VMEM((2 * rows, N * N + WINDOW), BF16),
    ]


def own_coefficients(val, cond, wide, key):
    return pl.pallas_call(
        own_kernel,
        out_shape=jax.ShapeDtypeStruct((2, 2, NG), F32),
        in_specs=[VM] * 5 + [SM, VM],
        out_specs=VM,
        scratch_shapes=scratch(2),
        compiler_params=pltpu.CompilerParams(vmem_limit_bytes=16 * 2**20),
        cost_estimate=pl.CostEstimate(flops=5 * 10**9, bytes_accessed=3 * 10**7, transcendentals=0),
    )(val, cond, *wide, key, key)


def coefficients(core, part, other, cond, wide, key, back, w, owned):
    return pl.pallas_call(
        rest_kernel,
        out_shape=(
            jax.ShapeDtypeStruct((32, 8, 640), BF16),
            jax.ShapeDtypeStruct((8, 8, 1280), BF16),
        ),
        in_specs=[SM] + [VM] * 6 + [SM] + [VM] * 4,
        out_specs=(VM, VM),
        scratch_shapes=scratch(6) + [pltpu.VMEM((2, 8, NG), F32)] * 2,
        compiler_params=pltpu.CompilerParams(vmem_limit_bytes=24 * 2**20),
        cost_estimate=pl.CostEstimate(flops=10**10, bytes_accessed=5 * 10**7, transcendentals=0),
    )(core, part, other, cond, *wide, key, key, back, w, owned)


def left_kernel(place, rows, l0, l1, l2, l3, turned, held, lk):
    for i, piece in enumerate((l0, l1, l2, l3)):
        held[2 * i : 2 * i + 2] = piece[...]

    def fill(k, _):
        r = rows[k]
        for u in range(4):
            pair = [held[place[2 * u + e], r].astype(F32) for e in range(2)]
            lk[pl.ds(pl.multiple_of(k * 64 + u * 16, 16), 16), :] = jnp.concatenate(pair, axis=0).astype(BF16)
        return 0

    lax.fori_loop(0, 16, fill, 0)
    turned[...] = lk[...].T


def left_matrix(place, rows, lefts):
    return pl.pallas_call(
        left_kernel,
        out_shape=jax.ShapeDtypeStruct((640, 1024), BF16),
        in_specs=[SM] * 2 + [VM] * 4,
        out_specs=VM,
        scratch_shapes=[pltpu.VMEM((8, 16, 8, 640), BF16), pltpu.VMEM((1024, 640), BF16)],
        compiler_params=pltpu.CompilerParams(vmem_limit_bytes=12 * 2**20),
    )(place, rows, *lefts)


def products(left, right):
    both = jnp.dot(left, right, preferred_element_type=F32)
    re, im = both[:320], both[320:]
    return re[:, :640] + im[:, 640:], im[:, :640] - re[:, 640:]


def early_kernel(left, r0, r1, r2, acc, rk):
    for i, piece in enumerate((r0, r1, r2)):
        rk[i * 256 : (i + 1) * 256] = piece[...]
    acc[0], acc[1] = products(left[:, :768], rk[...])


def late_kernel(core, left, r3, acc, mine, theirs):
    first = core[0] == 0
    chis = products(left[:, 768:], r3[...])
    for k in range(2):
        chi = acc[k] + chis[k]
        a, b = chi[:, :320], chi[:, 320:]
        cols = slice(k * 320, (k + 1) * 320)
        mine[:, cols] = jnp.where(first, a, b)
        theirs[:, cols] = jnp.where(first, b, a).astype(BF16)


def chi_tiles(core, place, rows, lefts, rights):
    left = left_matrix(place, rows, lefts)
    acc = pl.pallas_call(
        early_kernel,
        out_shape=jax.ShapeDtypeStruct((2, 320, 640), F32),
        in_specs=[VM] * 4,
        out_specs=VM,
        scratch_shapes=[pltpu.VMEM((768, 1280), BF16)],
        compiler_params=pltpu.CompilerParams(vmem_limit_bytes=20 * 2**20),
    )(left, *rights[:3])
    return pl.pallas_call(
        late_kernel,
        out_shape=(jax.ShapeDtypeStruct((320, 640), F32), jax.ShapeDtypeStruct((320, 640), BF16)),
        in_specs=[SM] + [VM] * 3,
        out_specs=(VM, VM),
        compiler_params=pltpu.CompilerParams(vmem_limit_bytes=20 * 2**20),
    )(core, left, rights[3], acc)


def device(z, y, x, c):
    return ((((z % 4) * 4 + y % 4) * 4 + x % 4) * 2 + (z % 8) // 4) * 2 + c


def send(values, target):
    pairs = [
        (device(z, y, x, c), device(*target(z, y, x, c)))
        for z in range(8)
        for y in range(4)
        for x in range(4)
        for c in range(2)
    ]
    return lax.ppermute(values, AXES, pairs)


def send_z(values, step):
    return send(values, lambda z, y, x, c: (z + step, y, x, c))


def send_core(values):
    return send(values, lambda z, y, x, c: (z, y, x, 1 - c))


def plane(axis, move):
    def target(z, y, x, c):
        if axis == c:
            return z, y, move(x), c
        return z, move(y), x, c

    return target


def outward(a):
    return a + 1 if a % 2 else a - 1


def inward(a):
    return a ^ 1


def ring(move):
    def target(z, y, x, c):
        return (move((z - c) % 8) + c) % 8, y, x, c

    return target


def pair_exchange(left):
    groups = []
    for c in range(2):
        for k in range(4):
            zs = [(2 * k + e + c) % 8 for e in range(2)]
            groups.append([device(z, y, x, c) for z in zs for y in range(4) for x in range(4)])
    got = lax.all_to_all(left, AXES, 0, 0, axis_index_groups=groups, tiled=True)
    return got.reshape(2, 16, 8, 640)


def assemble_kernel(tile, re, im):
    for f, out in enumerate((re, im)):
        parts = [tile[k, :, f * 320 : (f + 1) * 320].astype(F32) for k in range(4)]
        out[...] = jnp.concatenate(parts, axis=1)


def assemble(tile):
    return pl.pallas_call(
        assemble_kernel,
        out_shape=(jax.ShapeDtypeStruct((80, 1280), F32),) * 2,
        in_specs=[VM],
        out_specs=(VM, VM),
    )(tile)


def local(valence, conduction, valence_energy, conduction_energy, g_index):
    p, y, x, h, c = (lax.axis_index(a) for a in AXES)
    z = h * 4 + p
    core = jnp.reshape(c, (1,)).astype(jnp.int32)

    piece = lax.dynamic_index_in_dim(valence[0], c, 0, keepdims=False)
    part = jnp.concatenate(
        [
            send_z(piece, -1)[None],
            send(piece, lambda z, y, x, c: (z + 2 - 4 * c, y, x, c))[None],
            send_z(piece, 1)[None],
        ]
    )

    key, back = sort_waves(g_index.reshape(1, NG))

    energies = lax.dynamic_slice(jnp.tile(valence_energy, 2), (p,), (NV,))
    scale = math.sqrt(NV * 512)
    weight = 2.0 / ((energies[:, None] - conduction_energy[None, :]) * scale)

    wide = [jnp.asarray(t) for t in wide_tables()]
    owned = own_coefficients(valence, conduction, wide, key)
    part, owned = lax.optimization_barrier((part, owned))
    other = send_core(part)
    left, right = coefficients(
        core, part, other, conduction, wide, key, back, weight.reshape(8, 1), owned
    )

    right = lax.all_to_all(right, ("h", "p"), 0, 0, tiled=True).reshape(64, 1280)
    left, right = lax.optimization_barrier((left, right))
    left0 = pair_exchange(left)
    zz = (z - c) % 8
    left1 = send(left0, ring(outward))
    left2 = send(left1, ring(inward))
    left3 = send(left2, ring(outward))
    near = zz ^ 1
    one = (zz + 2 * (zz % 2) - 1) % 8
    two = (near + 2 * (near % 2) - 1) % 8
    three = ((one ^ 1) + 2 * ((one ^ 1) % 2) - 1) % 8
    held = jnp.stack([zz & 6, zz | 1, one & 6, one | 1, two & 6, two | 1, three & 6, three | 1])
    held = (held + c) % 8
    place = jnp.argmax(held[None, :] == jnp.arange(8)[:, None], axis=1).astype(jnp.int32)

    moves = (lambda i: i + 2, lambda i: i - 1, lambda i: i + 1)
    offsets = jnp.array([0, 2, 1, 3])
    four = jnp.concatenate([right] + [send(right, plane(0, move)) for move in moves])
    rights = [four] + [send(four, plane(1, move)) for move in moves]
    aa = jnp.tile((jnp.where(c == 0, x, y) + offsets) % 4, 4)
    bb = jnp.repeat((jnp.where(c == 0, y, x) + offsets) % 4, 4)
    rows = jnp.where(c == 0, bb * 4 + aa, aa * 4 + bb).astype(jnp.int32)

    mine, theirs = chi_tiles(core, place, rows, (left0, left1, left2, left3), rights)
    tile = (mine + send_core(theirs).astype(F32)).astype(BF16).reshape(4, 80, 640)
    return assemble(lax.all_to_all(tile, "p", 0, 0, tiled=True))


def solution(mesh):
    fine = Mesh(mesh.devices.reshape(4, 4, 4, 2, 2), AXES)
    bands = P(AXES)
    return jax.shard_map(
        local,
        mesh=fine,
        in_specs=(P("p"), bands, P(), bands, P()),
        out_specs=(P(("p", "y", "x"), ("h", "c")),) * 2,
        check_vma=False,
    )
```

```python
import functools
import math

import jax
import jax.numpy as jnp
import ml_dtypes
import numpy as np
from jax import lax
from jax.experimental import pallas as pl
from jax.experimental.pallas import tpu as pltpu
from jax.sharding import Mesh, PartitionSpec as P

NV = 4
N = 48
NG = 5120
F32 = jnp.float32
BF16 = jnp.bfloat16
WINDOW = 256
GROUP = 20
BUCKETS = 24
VM = pl.BlockSpec(memory_space=pltpu.VMEM)
SM = pl.BlockSpec(memory_space=pltpu.SMEM)
AXES = ("p", "y", "x", "h", "c")


def tables():
    k = np.arange(N)
    ang = (k[:, None] * k[None, :] % N).astype(np.float32) * np.float32(2.0 * math.pi / N)
    fac = np.float32(1.0 / math.sqrt(N))
    cos = (np.cos(ang) * fac).astype(ml_dtypes.bfloat16)
    sin = (np.sin(ang) * fac).astype(ml_dtypes.bfloat16)
    return cos, sin


def wide_tables():
    cos, sin = tables()
    cs = cos.astype(np.float32)
    sn = sin.astype(np.float32)
    eye8 = np.eye(8, dtype=np.float32)
    wz = np.zeros((2, 8, 48, 2, 48, 8), np.float32)
    for (f, g, tab) in ((0, 0, cs), (1, 0, sn), (0, 1, -sn), (1, 1, cs)):
        wz[f, :, :, g] = np.einsum("ab,kz->azkb", eye8, tab)
    wz = wz.reshape(768, 768)
    eye16 = np.eye(16, dtype=np.float32)
    wy = np.zeros((6, 16, 8, 2, 16, 24), np.float32)
    half = sn[:24].copy()
    half[0] = cs[24]
    for j, tab in enumerate((cs[:24], half)):
        wy[:, :, :, j] = np.einsum("ab,kmi->maibk", eye16, tab.reshape(24, 6, 8))
    wy = wy.reshape(768, 768)
    return wz.astype(ml_dtypes.bfloat16), wy.astype(ml_dtypes.bfloat16), cos, sin


def column_of(y, z):
    within = jnp.where(y < 24, y, jnp.where(y == 24, 0, N - y))
    return (z >> 4) * 768 + jnp.where(y < 24, 0, 384) + (z & 15) * 24 + within


def wave_keys(waves):
    x = ((waves.astype(F32) + 0.5) * (1.0 / (N * N))).astype(jnp.int32)
    rest = waves - x * (N * N)
    y = ((rest.astype(F32) + 0.5) * (1.0 / N)).astype(jnp.int32)
    key = (column_of(y, rest - y * N) << 6) | x
    starts = [(2 * h + c) * 1280 + p * 320 for h in range(2) for p in range(4) for c in range(2)]
    return jnp.concatenate([key[:, s : s + 320] for s in starts], axis=1)


def sort_kernel(waves, keys, place, held):
    key = wave_keys(waves[...])
    bucket = key >> 13
    slots = lax.broadcasted_iota(jnp.int32, (BUCKETS, 128), 0)
    before = jnp.zeros((BUCKETS, 128), F32)
    for k in range(40):
        mine = bucket[:, k * 128 : (k + 1) * 128]
        held[k] = jnp.where(slots == mine, 1.0, 0.0)
        before += jnp.where(mine < slots, 1.0, 0.0)
    upto = lax.broadcasted_iota(jnp.int32, (128, 128), 0) <= lax.broadcasted_iota(jnp.int32, (128, 128), 1)
    counts = jnp.dot(
        held[...].reshape(40 * BUCKETS, 128).astype(BF16),
        jnp.where(upto, 1.0, 0.0).astype(BF16),
        preferred_element_type=F32,
    ).reshape(40, BUCKETS, 128)
    base = jnp.sum(before, axis=1, keepdims=True) - 1.0
    for k in range(40):
        rank = jnp.sum(held[k] * (base + counts[k]), axis=0, keepdims=True)
        place[:, k * 128 : (k + 1) * 128] = rank.astype(jnp.int32)
        base = base + counts[k, :, 127:128]
    high = place[...] >> 7
    low = place[...] & 127
    at = lax.broadcasted_iota(jnp.int32, (40, NG), 0) == high
    parts = (bucket, (key >> 6) & 127, key & 63)
    rows = jnp.concatenate([jnp.where(at, v.astype(F32), 0.0) for v in parts], axis=0).astype(BF16)
    cols = jnp.where(lax.broadcasted_iota(jnp.int32, (128, NG), 0) == low, 1.0, 0.0).astype(BF16)
    moved = lax.dot_general(rows, cols, (((1,), (1,)), ((), ())), preferred_element_type=F32).astype(jnp.int32)
    keys[...] = (moved[0:40] << 13) | (moved[40:80] << 6) | moved[80:120]


def sort_waves(waves):
    return pl.pallas_call(
        sort_kernel,
        out_shape=(jax.ShapeDtypeStruct((40, 128), jnp.int32), jax.ShapeDtypeStruct((1, NG), jnp.int32)),
        in_specs=[VM],
        out_specs=(VM, VM),
        scratch_shapes=[pltpu.VMEM((40, BUCKETS, 128), F32)],
        compiler_params=pltpu.CompilerParams(vmem_limit_bytes=20 * 2**20),
        cost_estimate=pl.CostEstimate(flops=10**9, bytes_accessed=10**6, transcendentals=0),
    )(waves)


def densities(val, cond, cols, xs, k):
    for v in range(len(val)):
        vr, vi = val[v](cols)
        for c in range(2):
            cr = cond[c, 0, :, cols].astype(F32)
            ci = cond[c, 1, :, cols].astype(F32)
            rows = slice((v * 2 + c) * N, (v * 2 + c + 1) * N)
            xs[k, rows, 0:384] = (vr * cr + vi * ci).astype(BF16)
            xs[k, rows, 384:768] = (vr * ci - vi * cr).astype(BF16)


def sections(val, cond, wz, wy, xs, zs, s):
    count = zs.shape[1] // 2
    for i in range(6):
        densities(val, cond, slice(i * 384, (i + 1) * 384), xs, i % 2)
        out = jnp.dot(xs[i % 2], wz[...], preferred_element_type=F32).astype(BF16)
        for t in range(3):
            for f in range(2):
                zs[t, f * count : (f + 1) * count, i * 128 : (i + 1) * 128] = out[
                    :, f * 384 + t * 128 : f * 384 + (t + 1) * 128
                ]
    edge = lax.broadcasted_iota(jnp.int32, (1, 384), 1) % 24 == 0
    for t in range(3):
        cp = jnp.dot(zs[t], wy[:, :384], preferred_element_type=F32)
        sp = jnp.dot(zs[t], wy[:, 384:], preferred_element_type=F32)
        cre, cim, sre, sim = cp[:count], cp[count:], sp[:count], sp[count:]
        outs = (
            (jnp.where(edge, cre, cre + sim), jnp.where(edge, sre, cre - sim)),
            (jnp.where(edge, cim, cim - sre), jnp.where(edge, sim, cim + sre)),
        )
        for f in range(2):
            for e in range(2):
                cols = slice((t * 2 + e) * 384, (t * 2 + e + 1) * 384)
                s[f * count : (f + 1) * count, cols] = outs[f][e].astype(BF16)
    s[:, N * N :] = jnp.zeros((2 * count, WINDOW), BF16)


def select(s, tc, ts, starts, key, m, row):
    pairs = s.shape[0] // (2 * N)

    def step(group, _):
        todo = []
        keys = key[pl.ds(pl.multiple_of(group * 2 * GROUP, 8), 2 * GROUP), :]
        for u in range(GROUP):
            n = group * GROUP + u
            cols = pl.ds(pl.multiple_of(n * 256, 128), 256)
            waves = jnp.concatenate([keys[2 * u : 2 * u + 1], keys[2 * u + 1 : 2 * u + 2]], axis=1)
            column = waves >> 6
            kx = waves & 63
            hot = jnp.where(lax.broadcasted_iota(jnp.int32, (N, 256), 0) == kx, 1.0, 0.0).astype(BF16)
            co = jnp.dot(tc[...], hot, preferred_element_type=F32)
            si = jnp.dot(ts[...], hot, preferred_element_type=F32)
            low = starts[2 * n, 0] >> 13 << 7
            high = starts[2 * n + 1, 127] >> 6 | 127

            def window(base, column=column, co=co, si=si):
                rows = lax.broadcasted_iota(jnp.int32, (WINDOW, 256), 0)
                pick = jnp.where(rows == column - base, 1.0, 0.0).astype(BF16)
                part = s[:, pl.ds(pl.multiple_of(base, 128), WINDOW)]
                full = jnp.dot(part, pick, preferred_element_type=F32).reshape(2, pairs, N, 256)
                re = jnp.sum(full[0] * co + full[1] * si, axis=1)
                im = jnp.sum(full[1] * co - full[0] * si, axis=1)
                return re, im

            re, im = window(low)
            m[0, row : row + pairs, cols] = re
            m[1, row : row + pairs, cols] = im
            todo.append((window, low, high, cols))
        for window, low, high, cols in todo:

            def more(k, _, window=window, low=low, cols=cols):
                re, im = window(low + k * WINDOW)
                m[0, row : row + pairs, cols] += re
                m[1, row : row + pairs, cols] += im
                return 0

            lax.fori_loop(1, (high - low) // WINDOW + 1, more, 0)
        return 0

    lax.fori_loop(0, 20 // GROUP, step, 0)


def own_kernel(val, cond, wz, wy, tc, ts, starts, key, m, xs, zs, s):
    def band(cols):
        return val[0, 0, :, cols].astype(F32), val[0, 1, :, cols].astype(F32)

    sections([band], cond, wz, wy, xs, zs, s)
    select(s, tc, ts, starts, key, m, 0)


def rest_kernel(core, ve, ce, p0, p1, p2, o0, o1, o2, cond, wz, wy, tc, ts, starts, key, back, owned, left, right, xs, zs, s, m, mo):
    first = core[0] == 0

    def band(v):
        def read(cols):
            a = (p0, p1, p2)[v][:, cols].astype(F32)
            b = (o0, o1, o2)[v][:, cols].astype(F32)
            return jnp.where(first, a, b), jnp.where(first, b, a)

        return read

    sections([band(v) for v in range(3)], cond, wz, wy, xs, zs, s)
    select(s, tc, ts, starts, key, m, 2)
    m[:, 0:2, :] = owned[...]

    def unsort(group, _):
        for u in range(8):
            cols = pl.ds(pl.multiple_of((group * 8 + u) * 128, 128), 128)
            place = jnp.broadcast_to(back[:, cols], (8, 128))
            source = place >> 7
            lane = place & 127
            outs = [jnp.zeros((8, 128), F32)] * 2
            for k in range(40):
                hit = source == k
                for f in range(2):
                    got = jnp.take_along_axis(m[f, :, k * 128 : (k + 1) * 128], lane, axis=1)
                    outs[f] = jnp.where(hit, got, outs[f])
            for f in range(2):
                mo[f, :, cols] = outs[f]
        return 0

    lax.fori_loop(0, 5, unsort, 0)
    for z in range(8):
        for f in range(2):
            right[z, :, f * 640 : (f + 1) * 640] = mo[f, :, z * 640 : (z + 1) * 640].astype(BF16)
    pair = lax.broadcasted_iota(jnp.int32, (8, 1), 0)
    gap = jnp.zeros((8, 1), F32)
    for v in range(NV):
        for c in range(2):
            gap = jnp.where(pair == v * 2 + c, ve[(core[1] + v) & 3] - ce[c], gap)
    weight = 2.0 / (gap * math.sqrt(NV * 512))
    for r in range(16):
        parts = []
        for f in range(2):
            for b in range(4):
                lane = ((b // 2 * 4 + r // 4) * 2 + b % 2) * 320 + 80 * (r % 4)
                parts.append(mo[f, :, lane : lane + 80])
        block = (weight * jnp.concatenate(parts, axis=1)).astype(BF16)
        left[r] = block
        left[16 + r] = block


def scratch(pairs):
    rows = pairs * N
    return [
        pltpu.VMEM((2, rows, 768), BF16),
        pltpu.VMEM((3, 2 * rows, 768), BF16),
        pltpu.VMEM((2 * rows, N * N + WINDOW), BF16),
    ]


def own_coefficients(val, cond, wide, key):
    return pl.pallas_call(
        own_kernel,
        out_shape=jax.ShapeDtypeStruct((2, 2, NG), F32),
        in_specs=[VM] * 6 + [SM, VM],
        out_specs=VM,
        scratch_shapes=scratch(2),
        compiler_params=pltpu.CompilerParams(vmem_limit_bytes=16 * 2**20),
        cost_estimate=pl.CostEstimate(flops=5 * 10**9, bytes_accessed=3 * 10**7, transcendentals=0),
    )(val, cond, *wide, key, key)


def coefficients(core, ve, ce, part, other, cond, wide, key, back, owned):
    return pl.pallas_call(
        rest_kernel,
        out_shape=(
            jax.ShapeDtypeStruct((32, 8, 640), BF16),
            jax.ShapeDtypeStruct((8, 8, 1280), BF16),
        ),
        in_specs=[SM] * 3 + [VM] * 11 + [SM] + [VM] * 3,
        out_specs=(VM, VM),
        scratch_shapes=scratch(6) + [pltpu.VMEM((2, 8, NG), F32)] * 2,
        compiler_params=pltpu.CompilerParams(vmem_limit_bytes=24 * 2**20),
        cost_estimate=pl.CostEstimate(flops=10**10, bytes_accessed=5 * 10**7, transcendentals=0),
    )(core, ve, ce, *part, *other, cond, *wide, key, key, back, owned)


def left_kernel(place, rows, l0, l1, l2, l3, turned, held, lk):
    for i, piece in enumerate((l0, l1, l2, l3)):
        held[2 * i : 2 * i + 2] = piece[...]

    def fill(k, _):
        r = rows[k]
        for u in range(4):
            pair = [held[place[2 * u + e], r].astype(F32) for e in range(2)]
            lk[pl.ds(pl.multiple_of(k * 64 + u * 16, 16), 16), :] = jnp.concatenate(pair, axis=0).astype(BF16)
        return 0

    lax.fori_loop(0, 16, fill, 0)
    turned[...] = lk[...].T


def left_matrix(place, rows, lefts):
    return pl.pallas_call(
        left_kernel,
        out_shape=jax.ShapeDtypeStruct((640, 1024), BF16),
        in_specs=[SM] * 2 + [VM] * 4,
        out_specs=VM,
        scratch_shapes=[pltpu.VMEM((8, 16, 8, 640), BF16), pltpu.VMEM((1024, 640), BF16)],
        compiler_params=pltpu.CompilerParams(vmem_limit_bytes=12 * 2**20),
    )(place, rows, *lefts)


def products(left, right):
    both = jnp.dot(left, right, preferred_element_type=F32)
    re, im = both[:320], both[320:]
    return re[:, :640] + im[:, 640:], im[:, :640] - re[:, 640:]


def early_kernel(left, r0, r1, r2, acc, rk):
    for i, piece in enumerate((r0, r1, r2)):
        rk[i * 256 : (i + 1) * 256] = piece[...]
    acc[0], acc[1] = products(left[:, :768], rk[...])


def late_kernel(core, left, r3, acc, mine, theirs):
    first = core[0] == 0
    chis = products(left[:, 768:], r3[...])
    for k in range(2):
        chi = acc[k] + chis[k]
        a, b = chi[:, :320], chi[:, 320:]
        cols = slice(k * 320, (k + 1) * 320)
        mine[:, cols] = jnp.where(first, a, b)
        theirs[:, cols] = jnp.where(first, b, a).astype(BF16)


def chi_tiles(core, place, rows, lefts, rights):
    left = left_matrix(place, rows, lefts)
    acc = pl.pallas_call(
        early_kernel,
        out_shape=jax.ShapeDtypeStruct((2, 320, 640), F32),
        in_specs=[VM] * 4,
        out_specs=VM,
        scratch_shapes=[pltpu.VMEM((768, 1280), BF16)],
        compiler_params=pltpu.CompilerParams(vmem_limit_bytes=20 * 2**20),
    )(left, *rights[:3])
    return pl.pallas_call(
        late_kernel,
        out_shape=(jax.ShapeDtypeStruct((320, 640), F32), jax.ShapeDtypeStruct((320, 640), BF16)),
        in_specs=[SM] + [VM] * 3,
        out_specs=(VM, VM),
        compiler_params=pltpu.CompilerParams(vmem_limit_bytes=20 * 2**20),
    )(core, left, rights[3], acc)


def device(z, y, x, c):
    return ((((z % 4) * 4 + y % 4) * 4 + x % 4) * 2 + (z % 8) // 4) * 2 + c


def send(values, target):
    pairs = [
        (device(z, y, x, c), device(*target(z, y, x, c)))
        for z in range(8)
        for y in range(4)
        for x in range(4)
        for c in range(2)
    ]
    return lax.ppermute(values, AXES, pairs)


def send_z(values, step):
    return send(values, lambda z, y, x, c: (z + step, y, x, c))


def send_core(values):
    return send(values, lambda z, y, x, c: (z, y, x, 1 - c))


def plane(axis, move):
    def target(z, y, x, c):
        if axis == c:
            return z, y, move(x), c
        return z, move(y), x, c

    return target


def outward(a):
    return a + 1 if a % 2 else a - 1


def inward(a):
    return a ^ 1


def ring(move):
    def target(z, y, x, c):
        return (move((z - c) % 8) + c) % 8, y, x, c

    return target


def pair_exchange(left):
    groups = []
    for c in range(2):
        for k in range(4):
            zs = [(2 * k + e + c) % 8 for e in range(2)]
            groups.append([device(z, y, x, c) for z in zs for y in range(4) for x in range(4)])
    got = lax.all_to_all(left, AXES, 0, 0, axis_index_groups=groups, tiled=True)
    return got.reshape(2, 16, 8, 640)


def assemble_kernel(tile, re, im):
    for f, out in enumerate((re, im)):
        parts = [tile[k, :, f * 320 : (f + 1) * 320].astype(F32) for k in range(4)]
        out[...] = jnp.concatenate(parts, axis=1)


def assemble(tile):
    return pl.pallas_call(
        assemble_kernel,
        out_shape=(jax.ShapeDtypeStruct((80, 1280), F32),) * 2,
        in_specs=[VM],
        out_specs=(VM, VM),
    )(tile)


def local(valence, conduction, valence_energy, conduction_energy, g_index):
    p, y, x, h, c = (lax.axis_index(a) for a in AXES)
    z = h * 4 + p
    core = jnp.reshape(c, (1,)).astype(jnp.int32)

    piece = lax.dynamic_index_in_dim(valence[0], c, 0, keepdims=False)
    part = [
        send_z(piece, -1),
        send(piece, lambda z, y, x, c: (z + 2 - 4 * c, y, x, c)),
        send_z(piece, 1),
    ]

    key, back = sort_waves(g_index.reshape(1, NG))

    wide = [jnp.asarray(t) for t in wide_tables()]
    owned = own_coefficients(valence, conduction, wide, key)
    part, owned = lax.optimization_barrier((part, owned))
    other = [send_core(v) for v in part]
    mine = jnp.stack([c, p]).astype(jnp.int32)
    left, right = coefficients(
        mine, valence_energy, conduction_energy, part, other, conduction, wide, key, back, owned
    )

    right = lax.all_to_all(right, ("h", "p"), 0, 0, tiled=True).reshape(64, 1280)
    left, right = lax.optimization_barrier((left, right))
    left0 = pair_exchange(left)
    zz = (z - c) % 8
    left1 = send(left0, ring(outward))
    left2 = send(left1, ring(inward))
    left3 = send(left2, ring(outward))
    near = zz ^ 1
    one = (zz + 2 * (zz % 2) - 1) % 8
    two = (near + 2 * (near % 2) - 1) % 8
    three = ((one ^ 1) + 2 * ((one ^ 1) % 2) - 1) % 8
    held = jnp.stack([zz & 6, zz | 1, one & 6, one | 1, two & 6, two | 1, three & 6, three | 1])
    held = (held + c) % 8
    place = jnp.argmax(held[None, :] == jnp.arange(8)[:, None], axis=1).astype(jnp.int32)

    moves = (lambda i: i + 2, lambda i: i - 1, lambda i: i + 1)
    offsets = jnp.array([0, 2, 1, 3])
    four = jnp.concatenate([right] + [send(right, plane(0, move)) for move in moves])
    rights = [four] + [send(four, plane(1, move)) for move in moves]
    aa = jnp.tile((jnp.where(c == 0, x, y) + offsets) % 4, 4)
    bb = jnp.repeat((jnp.where(c == 0, y, x) + offsets) % 4, 4)
    rows = jnp.where(c == 0, bb * 4 + aa, aa * 4 + bb).astype(jnp.int32)

    mine, theirs = chi_tiles(core, place, rows, (left0, left1, left2, left3), rights)
    tile = (mine + send_core(theirs).astype(F32)).astype(BF16).reshape(4, 80, 640)
    return assemble(lax.all_to_all(tile, "p", 0, 0, tiled=True))


def solution(mesh):
    fine = Mesh(mesh.devices.reshape(4, 4, 4, 2, 2), AXES)
    bands = P(AXES)
    return jax.shard_map(
        local,
        mesh=fine,
        in_specs=(P("p"), bands, P(), bands, P()),
        out_specs=(P(("p", "y", "x"), ("h", "c")),) * 2,
        check_vma=False,
    )
```

```python
import functools
import math

import jax
import jax.numpy as jnp
import ml_dtypes
import numpy as np
from jax import lax
from jax.experimental import pallas as pl
from jax.experimental.pallas import tpu as pltpu
from jax.sharding import Mesh, PartitionSpec as P

NV = 4
N = 48
NG = 5120
F32 = jnp.float32
BF16 = jnp.bfloat16
WINDOW = 256
GROUP = 20
BUCKETS = 24
VM = pl.BlockSpec(memory_space=pltpu.VMEM)
SM = pl.BlockSpec(memory_space=pltpu.SMEM)
AXES = ("p", "y", "x", "h", "c")


def tables():
    k = np.arange(N)
    ang = (k[:, None] * k[None, :] % N).astype(np.float32) * np.float32(2.0 * math.pi / N)
    fac = np.float32(1.0 / math.sqrt(N))
    cos = (np.cos(ang) * fac).astype(ml_dtypes.bfloat16)
    sin = (np.sin(ang) * fac).astype(ml_dtypes.bfloat16)
    return cos, sin


def wide_tables():
    cos, sin = tables()
    cs = cos.astype(np.float32)
    sn = sin.astype(np.float32)
    eye8 = np.eye(8, dtype=np.float32)
    wz = np.zeros((2, 8, 48, 2, 48, 8), np.float32)
    for (f, g, tab) in ((0, 0, cs), (1, 0, sn), (0, 1, -sn), (1, 1, cs)):
        wz[f, :, :, g] = np.einsum("ab,kz->azkb", eye8, tab)
    wz = wz.reshape(768, 768)
    eye16 = np.eye(16, dtype=np.float32)
    wy = np.zeros((6, 16, 8, 2, 16, 24), np.float32)
    half = sn[:24].copy()
    half[0] = cs[24]
    for j, tab in enumerate((cs[:24], half)):
        wy[:, :, :, j] = np.einsum("ab,kmi->maibk", eye16, tab.reshape(24, 6, 8))
    wy = wy.reshape(768, 768)
    return wz.astype(ml_dtypes.bfloat16), wy.astype(ml_dtypes.bfloat16), cos, sin


def column_of(y, z):
    within = jnp.where(y < 24, y, jnp.where(y == 24, 0, N - y))
    return (z >> 4) * 768 + jnp.where(y < 24, 0, 384) + (z & 15) * 24 + within


def wave_keys(waves):
    x = ((waves.astype(F32) + 0.5) * (1.0 / (N * N))).astype(jnp.int32)
    rest = waves - x * (N * N)
    y = ((rest.astype(F32) + 0.5) * (1.0 / N)).astype(jnp.int32)
    key = (column_of(y, rest - y * N) << 6) | x
    starts = [(2 * h + c) * 1280 + p * 320 for h in range(2) for p in range(4) for c in range(2)]
    return jnp.concatenate([key[:, s : s + 320] for s in starts], axis=1)


def sort_kernel(waves, keys, place, held):
    key = wave_keys(waves[...])
    bucket = key >> 13
    slots = lax.broadcasted_iota(jnp.int32, (BUCKETS, 128), 0)
    before = jnp.zeros((BUCKETS, 128), F32)
    for k in range(40):
        mine = bucket[:, k * 128 : (k + 1) * 128]
        held[k] = jnp.where(slots == mine, 1.0, 0.0)
        before += jnp.where(mine < slots, 1.0, 0.0)
    upto = lax.broadcasted_iota(jnp.int32, (128, 128), 0) <= lax.broadcasted_iota(jnp.int32, (128, 128), 1)
    counts = jnp.dot(
        held[...].reshape(40 * BUCKETS, 128).astype(BF16),
        jnp.where(upto, 1.0, 0.0).astype(BF16),
        preferred_element_type=F32,
    ).reshape(40, BUCKETS, 128)
    base = jnp.sum(before, axis=1, keepdims=True) - 1.0
    for k in range(40):
        rank = jnp.sum(held[k] * (base + counts[k]), axis=0, keepdims=True)
        place[:, k * 128 : (k + 1) * 128] = rank.astype(jnp.int32)
        base = base + counts[k, :, 127:128]
    high = place[...] >> 7
    low = place[...] & 127
    at = lax.broadcasted_iota(jnp.int32, (40, NG), 0) == high
    parts = (bucket, (key >> 6) & 127, key & 63)
    rows = jnp.concatenate([jnp.where(at, v.astype(F32), 0.0) for v in parts], axis=0).astype(BF16)
    cols = jnp.where(lax.broadcasted_iota(jnp.int32, (128, NG), 0) == low, 1.0, 0.0).astype(BF16)
    moved = lax.dot_general(rows, cols, (((1,), (1,)), ((), ())), preferred_element_type=F32).astype(jnp.int32)
    keys[...] = (moved[0:40] << 13) | (moved[40:80] << 6) | moved[80:120]


def sort_waves(waves):
    return pl.pallas_call(
        sort_kernel,
        out_shape=(jax.ShapeDtypeStruct((40, 128), jnp.int32), jax.ShapeDtypeStruct((1, NG), jnp.int32)),
        in_specs=[VM],
        out_specs=(VM, VM),
        scratch_shapes=[pltpu.VMEM((40, BUCKETS, 128), F32)],
        compiler_params=pltpu.CompilerParams(vmem_limit_bytes=20 * 2**20),
        cost_estimate=pl.CostEstimate(flops=10**9, bytes_accessed=10**6, transcendentals=0),
    )(waves)


def densities(val, cond, cols, xs, k):
    for v in range(len(val)):
        vr, vi = val[v](cols)
        for c in range(2):
            cr = cond[c, 0, :, cols].astype(F32)
            ci = cond[c, 1, :, cols].astype(F32)
            rows = slice((v * 2 + c) * N, (v * 2 + c + 1) * N)
            xs[k, rows, 0:384] = (vr * cr + vi * ci).astype(BF16)
            xs[k, rows, 384:768] = (vr * ci - vi * cr).astype(BF16)


def sections(val, cond, wz, wy, xs, zs, s):
    count = zs.shape[1] // 2
    for i in range(6):
        densities(val, cond, slice(i * 384, (i + 1) * 384), xs, i % 2)
        out = jnp.dot(xs[i % 2], wz[...], preferred_element_type=F32).astype(BF16)
        for t in range(3):
            for f in range(2):
                zs[t, f * count : (f + 1) * count, i * 128 : (i + 1) * 128] = out[
                    :, f * 384 + t * 128 : f * 384 + (t + 1) * 128
                ]
    edge = lax.broadcasted_iota(jnp.int32, (1, 384), 1) % 24 == 0
    for t in range(3):
        cp = jnp.dot(zs[t], wy[:, :384], preferred_element_type=F32)
        sp = jnp.dot(zs[t], wy[:, 384:], preferred_element_type=F32)
        cre, cim, sre, sim = cp[:count], cp[count:], sp[:count], sp[count:]
        outs = (
            (jnp.where(edge, cre, cre + sim), jnp.where(edge, sre, cre - sim)),
            (jnp.where(edge, cim, cim - sre), jnp.where(edge, sim, cim + sre)),
        )
        for f in range(2):
            for e in range(2):
                cols = slice((t * 2 + e) * 384, (t * 2 + e + 1) * 384)
                s[f * count : (f + 1) * count, cols] = outs[f][e].astype(BF16)
    s[:, N * N :] = jnp.zeros((2 * count, WINDOW), BF16)


def select(s, tc, ts, starts, key, m, row):
    pairs = s.shape[0] // (2 * N)

    def step(group, _):
        todo = []
        keys = key[pl.ds(pl.multiple_of(group * 2 * GROUP, 8), 2 * GROUP), :]
        for u in range(GROUP):
            n = group * GROUP + u
            cols = pl.ds(pl.multiple_of(n * 256, 128), 256)
            waves = jnp.concatenate([keys[2 * u : 2 * u + 1], keys[2 * u + 1 : 2 * u + 2]], axis=1)
            column = waves >> 6
            kx = waves & 63
            hot = jnp.where(lax.broadcasted_iota(jnp.int32, (N, 256), 0) == kx, 1.0, 0.0).astype(BF16)
            co = jnp.dot(tc[...], hot, preferred_element_type=F32)
            si = jnp.dot(ts[...], hot, preferred_element_type=F32)
            low = starts[2 * n, 0] >> 13 << 7
            high = starts[2 * n + 1, 127] >> 6 | 127

            def window(base, column=column, co=co, si=si):
                rows = lax.broadcasted_iota(jnp.int32, (WINDOW, 256), 0)
                pick = jnp.where(rows == column - base, 1.0, 0.0).astype(BF16)
                part = s[:, pl.ds(pl.multiple_of(base, 128), WINDOW)]
                full = jnp.dot(part, pick, preferred_element_type=F32).reshape(2, pairs, N, 256)
                re = jnp.sum(full[0] * co + full[1] * si, axis=1)
                im = jnp.sum(full[1] * co - full[0] * si, axis=1)
                return re, im

            re, im = window(low)
            m[0, row : row + pairs, cols] = re
            m[1, row : row + pairs, cols] = im
            todo.append((window, low, high, cols))
        for window, low, high, cols in todo:

            def more(k, _, window=window, low=low, cols=cols):
                re, im = window(low + k * WINDOW)
                m[0, row : row + pairs, cols] += re
                m[1, row : row + pairs, cols] += im
                return 0

            lax.fori_loop(1, (high - low) // WINDOW + 1, more, 0)
        return 0

    lax.fori_loop(0, 20 // GROUP, step, 0)


def own_kernel(val, cond, wz, wy, tc, ts, starts, key, m, xs, zs, s):
    def band(cols):
        return val[0, 0, :, cols].astype(F32), val[0, 1, :, cols].astype(F32)

    sections([band], cond, wz, wy, xs, zs, s)
    select(s, tc, ts, starts, key, m, 0)


def rest_kernel(core, ve, ce, p0, p1, p2, o0, o1, o2, cond, wz, wy, tc, ts, starts, key, back, owned, left, right, xs, zs, s, m, mo):
    first = core[0] == 0

    def band(v):
        def read(cols):
            a = (p0, p1, p2)[v][:, cols].astype(F32)
            b = (o0, o1, o2)[v][:, cols].astype(F32)
            return jnp.where(first, a, b), jnp.where(first, b, a)

        return read

    sections([band(v) for v in range(3)], cond, wz, wy, xs, zs, s)
    select(s, tc, ts, starts, key, m, 2)
    m[:, 0:2, :] = owned[...]

    def unsort(group, _):
        for u in range(8):
            cols = pl.ds(pl.multiple_of((group * 8 + u) * 128, 128), 128)
            place = jnp.broadcast_to(back[:, cols], (8, 128))
            source = place >> 7
            lane = place & 127
            outs = [jnp.zeros((8, 128), F32)] * 2
            for k in range(40):
                hit = source == k
                for f in range(2):
                    got = jnp.take_along_axis(m[f, :, k * 128 : (k + 1) * 128], lane, axis=1)
                    outs[f] = jnp.where(hit, got, outs[f])
            for f in range(2):
                mo[f, :, cols] = outs[f]
        return 0

    lax.fori_loop(0, 5, unsort, 0)
    for z in range(8):
        for f in range(2):
            right[z, :, f * 640 : (f + 1) * 640] = mo[f, :, z * 640 : (z + 1) * 640].astype(BF16)
    pair = lax.broadcasted_iota(jnp.int32, (8, 1), 0)
    gap = jnp.zeros((8, 1), F32)
    for v in range(NV):
        for c in range(2):
            gap = jnp.where(pair == v * 2 + c, ve[(core[1] + v) & 3] - ce[c], gap)
    weight = 2.0 / (gap * math.sqrt(NV * 512))
    for r in range(16):
        parts = []
        for f in range(2):
            for b in range(4):
                lane = ((b // 2 * 4 + r // 4) * 2 + b % 2) * 320 + 80 * (r % 4)
                parts.append(mo[f, :, lane : lane + 80])
        block = (weight * jnp.concatenate(parts, axis=1)).astype(BF16)
        left[r] = block
        left[16 + r] = block


def scratch(pairs):
    rows = pairs * N
    return [
        pltpu.VMEM((2, rows, 768), BF16),
        pltpu.VMEM((3, 2 * rows, 768), BF16),
        pltpu.VMEM((2 * rows, N * N + WINDOW), BF16),
    ]


def own_coefficients(val, cond, wide, key):
    return pl.pallas_call(
        own_kernel,
        out_shape=jax.ShapeDtypeStruct((2, 2, NG), F32),
        in_specs=[VM] * 6 + [SM, VM],
        out_specs=VM,
        scratch_shapes=scratch(2),
        compiler_params=pltpu.CompilerParams(vmem_limit_bytes=16 * 2**20),
        cost_estimate=pl.CostEstimate(flops=5 * 10**9, bytes_accessed=3 * 10**7, transcendentals=0),
    )(val, cond, *wide, key, key)


def coefficients(core, ve, ce, part, other, cond, wide, key, back, owned):
    return pl.pallas_call(
        rest_kernel,
        out_shape=(
            jax.ShapeDtypeStruct((32, 8, 640), BF16),
            jax.ShapeDtypeStruct((8, 8, 1280), BF16),
        ),
        in_specs=[SM] * 3 + [VM] * 11 + [SM] + [VM] * 3,
        out_specs=(VM, VM),
        scratch_shapes=scratch(6) + [pltpu.VMEM((2, 8, NG), F32)] * 2,
        compiler_params=pltpu.CompilerParams(vmem_limit_bytes=24 * 2**20),
        cost_estimate=pl.CostEstimate(flops=10**10, bytes_accessed=5 * 10**7, transcendentals=0),
    )(core, ve, ce, *part, *other, cond, *wide, key, key, back, owned)


def left_kernel(place, rows, l0, l1, l2, l3, turned, held, lk):
    for i, piece in enumerate((l0, l1, l2, l3)):
        held[2 * i : 2 * i + 2] = piece[...]

    def fill(k, _):
        r = rows[k]
        for u in range(4):
            pair = [held[place[2 * u + e], r].astype(F32) for e in range(2)]
            lk[pl.ds(pl.multiple_of(k * 64 + u * 16, 16), 16), :] = jnp.concatenate(pair, axis=0).astype(BF16)
        return 0

    lax.fori_loop(0, 16, fill, 0)
    turned[...] = lk[...].T


def left_matrix(place, rows, lefts):
    return pl.pallas_call(
        left_kernel,
        out_shape=jax.ShapeDtypeStruct((640, 1024), BF16),
        in_specs=[SM] * 2 + [VM] * 4,
        out_specs=VM,
        scratch_shapes=[pltpu.VMEM((8, 16, 8, 640), BF16), pltpu.VMEM((1024, 640), BF16)],
        compiler_params=pltpu.CompilerParams(vmem_limit_bytes=12 * 2**20),
    )(place, rows, *lefts)


def products(left, right):
    both = jnp.dot(left, right, preferred_element_type=F32)
    re, im = both[:320], both[320:]
    return re[:, :640] + im[:, 640:], im[:, :640] - re[:, 640:]


def early_kernel(left, r0, r1, r2, acc, rk):
    for i, piece in enumerate((r0, r1, r2)):
        rk[i * 256 : (i + 1) * 256] = piece[...]
    acc[0], acc[1] = products(left[:, :768], rk[...])


def late_kernel(core, left, r3, acc, mine, theirs):
    first = core[0] == 0
    chis = products(left[:, 768:], r3[...])
    for k in range(2):
        chi = acc[k] + chis[k]
        a, b = chi[:, :320], chi[:, 320:]
        cols = slice(k * 320, (k + 1) * 320)
        mine[:, cols] = jnp.where(first, a, b)
        theirs[:, cols] = jnp.where(first, b, a).astype(BF16)


def chi_tiles(core, place, rows, lefts, rights):
    left = left_matrix(place, rows, lefts)
    acc = pl.pallas_call(
        early_kernel,
        out_shape=jax.ShapeDtypeStruct((2, 320, 640), F32),
        in_specs=[VM] * 4,
        out_specs=VM,
        scratch_shapes=[pltpu.VMEM((768, 1280), BF16)],
        compiler_params=pltpu.CompilerParams(vmem_limit_bytes=20 * 2**20),
    )(left, *rights[:3])
    return pl.pallas_call(
        late_kernel,
        out_shape=(jax.ShapeDtypeStruct((320, 640), F32), jax.ShapeDtypeStruct((320, 640), BF16)),
        in_specs=[SM] + [VM] * 3,
        out_specs=(VM, VM),
        compiler_params=pltpu.CompilerParams(vmem_limit_bytes=20 * 2**20),
    )(core, left, rights[3], acc)


def device(z, y, x, c):
    return ((((z % 4) * 4 + y % 4) * 4 + x % 4) * 2 + (z % 8) // 4) * 2 + c


def send(values, target):
    pairs = [
        (device(z, y, x, c), device(*target(z, y, x, c)))
        for z in range(8)
        for y in range(4)
        for x in range(4)
        for c in range(2)
    ]
    return lax.ppermute(values, AXES, pairs)


def send_z(values, step):
    return send(values, lambda z, y, x, c: (z + step, y, x, c))


def send_core(values):
    return send(values, lambda z, y, x, c: (z, y, x, 1 - c))


def plane(axis, move):
    def target(z, y, x, c):
        if axis == c:
            return z, y, move(x), c
        return z, move(y), x, c

    return target


def outward(a):
    return a + 1 if a % 2 else a - 1


def inward(a):
    return a ^ 1


def ring(move):
    def target(z, y, x, c):
        return (move((z - c) % 8) + c) % 8, y, x, c

    return target


def pair_exchange(left):
    groups = []
    for c in range(2):
        for k in range(4):
            zs = [(2 * k + e + c) % 8 for e in range(2)]
            groups.append([device(z, y, x, c) for z in zs for y in range(4) for x in range(4)])
    got = lax.all_to_all(left, AXES, 0, 0, axis_index_groups=groups, tiled=True)
    return got.reshape(2, 16, 8, 640)


def assemble_kernel(tile, re, im):
    for f, out in enumerate((re, im)):
        parts = [tile[k, :, f * 320 : (f + 1) * 320].astype(F32) for k in range(4)]
        out[...] = jnp.concatenate(parts, axis=1)


def assemble(tile):
    return pl.pallas_call(
        assemble_kernel,
        out_shape=(jax.ShapeDtypeStruct((80, 1280), F32),) * 2,
        in_specs=[VM],
        out_specs=(VM, VM),
    )(tile)


def local(valence, conduction, valence_energy, conduction_energy, g_index):
    p, y, x, h, c = (lax.axis_index(a) for a in AXES)
    z = h * 4 + p
    core = jnp.reshape(c, (1,)).astype(jnp.int32)

    piece = lax.dynamic_index_in_dim(valence[0], c, 0, keepdims=False)
    part = [
        send_z(piece, -1),
        send(piece, lambda z, y, x, c: (z + 2 - 4 * c, y, x, c)),
        send_z(piece, 1),
    ]

    key, back = sort_waves(g_index.reshape(1, NG))

    wide = [jnp.asarray(t) for t in wide_tables()]
    owned = own_coefficients(valence, conduction, wide, key)
    part, owned = lax.optimization_barrier((part, owned))
    other = [send_core(v) for v in part]
    mine = jnp.stack([c, p]).astype(jnp.int32)
    left, right = coefficients(
        mine, valence_energy, conduction_energy, part, other, conduction, wide, key, back, owned
    )

    right = lax.all_to_all(right, ("h", "p"), 0, 0, tiled=True).reshape(64, 1280)
    left, right = lax.optimization_barrier((left, right))
    left0 = pair_exchange(left)
    zz = (z - c) % 8
    left1 = send(left0, ring(outward))
    left2 = send(left1, ring(inward))
    left3 = send(left2, ring(outward))
    near = zz ^ 1
    one = (zz + 2 * (zz % 2) - 1) % 8
    two = (near + 2 * (near % 2) - 1) % 8
    three = ((one ^ 1) + 2 * ((one ^ 1) % 2) - 1) % 8
    held = jnp.stack([zz & 6, zz | 1, one & 6, one | 1, two & 6, two | 1, three & 6, three | 1])
    held = (held + c) % 8
    place = jnp.argmax(held[None, :] == jnp.arange(8)[:, None], axis=1).astype(jnp.int32)

    moves = (lambda i: i + 2, lambda i: i + 1, lambda i: i - 1)
    offsets = jnp.array([0, 2, 3, 1])
    four = jnp.concatenate([right] + [send(right, plane(0, move)) for move in moves])
    rights = [four] + [send(four, plane(1, move)) for move in moves]
    aa = jnp.tile((jnp.where(c == 0, x, y) + offsets) % 4, 4)
    bb = jnp.repeat((jnp.where(c == 0, y, x) + offsets) % 4, 4)
    rows = jnp.where(c == 0, bb * 4 + aa, aa * 4 + bb).astype(jnp.int32)

    mine, theirs = chi_tiles(core, place, rows, (left0, left1, left2, left3), rights)
    tile = (mine + send_core(theirs).astype(F32)).astype(BF16).reshape(4, 80, 640)
    return assemble(lax.all_to_all(tile, "p", 0, 0, tiled=True))


def solution(mesh):
    fine = Mesh(mesh.devices.reshape(4, 4, 4, 2, 2), AXES)
    bands = P(AXES)
    return jax.shard_map(
        local,
        mesh=fine,
        in_specs=(P("p"), bands, P(), bands, P()),
        out_specs=(P(("p", "y", "x"), ("h", "c")),) * 2,
        check_vma=False,
    )
```
